128 devices in a mesh: seq: 8 (over x_lo, y), head: 16 (over z, x_hi, core).
Axes of the slice: x: 4 (x_hi: 2, x_lo: 2; x = x_hi * 2 + x_lo), y: 4, z: 4, core: 2. Of those that a mesh axis runs over, the one named last changes fastest.
Arguments:
- queries: bfloat16 [4096, 8192], P('seq', 'head'), may hold values from -150 to 150
- keys: bfloat16 [4096, 1024], P('seq'), may hold values from -4 to 4
- values: bfloat16 [4096, 1024], P('seq'), may hold values from -6 to 6
- length: int32 [1], replicated, may hold values from 3585 to 4096
- mixer_values: bfloat16 [4096, 1024], P('seq'), may hold values from -6 to 6
- mixer_keys: bfloat16 [4096, 1024], P('seq'), may hold values from -6 to 6
- mixer_queries: bfloat16 [4096, 8192], P('seq', 'head'), may hold values from -0.5 to 0.5
- gate_values: bfloat16 [4096, 8192], P('seq', 'head'), may hold values from -6 to 6
- step_size: float32 [64, 4096], P('head', 'seq'), may hold values from 0.025 to 0.4
- decay_rate: float32 [64], P('head'), as said below
- skip_gain: float32 [64], P('head'), may hold values from 0.5 to 1.5
- out_weight: bfloat16 [8192, 8192], P('head'), may hold values from -0.0625 to 0.0625
Outputs:
- attn_heads: bfloat16 [4096, 8192], P('seq', 'head')
- ssm_out: bfloat16 [4096, 8192], P('seq', 'head')
- final_states: float32 [64, 128, 128], P('head', 'seq')
The draws below stay inside these ranges and needn't reach their ends.
Inputs may be any that keep to these rules, and one draw needn't show every extreme that they name: `decay_rate`: positive.
All inputs are finite; a program needn't handle non-finite values.
Results may differ from the reference program's by a relative error of at most 0.022.
Values may be sent and summed in bfloat16 or wider, within the bound.
No kernel may reach another device: no remote copies, remote signals or barrier semaphores. Data moves between devices by JAX's collectives and lax.ppermute only.
A program may use at most 128 MiB of HBM per device.

```python
import math
import jax
import jax.numpy as jnp
import numpy as np
from jax import lax

H = 64
KVH = 8
XG = 8
HD = 128
NST = 128
D = 8192
TOK_DEV = 512
SEQLEN = 4096


def pair_draw(key):
    key_base, key_query, key_pick = jax.random.split(key, 3)
    base_keys = jnp.clip(jax.random.normal(key_base, (SEQLEN, KVH, HD), jnp.float32), -4.0, 4.0)
    base_queries = jnp.clip(jax.random.normal(key_query, (SEQLEN, H, HD), jnp.float32), -4.0, 4.0)
    pick_one, pick_two, pick_three = jax.random.split(key_pick, 3)
    half_len = SEQLEN // 2
    query_rows = jax.random.randint(pick_one, (16,), half_len, SEQLEN)
    key_rows = jax.random.randint(pick_two, (16,), 0, half_len)
    offsets = jax.random.randint(pick_three, (16,), 1, half_len)
    twin_rows = (key_rows + offsets) % half_len
    base_keys = base_keys.at[twin_rows].set(base_keys[twin_rows])
    base_queries = base_queries.at[query_rows].set(base_queries[query_rows])
    return (base_queries.reshape(SEQLEN, H * HD), base_keys.reshape(SEQLEN, KVH * HD))


def draw_queries(key, part):
    return pair_draw(key)[0].astype(jnp.bfloat16)


def draw_keys(key, part):
    return pair_draw(key)[1].astype(jnp.bfloat16)


def draw_step_size(key, part):
    key = jax.random.fold_in(key, 11)
    key_rough, key_block = jax.random.split(key)
    rough = jnp.exp(jax.random.uniform(key_rough, (H, SEQLEN), jnp.float32, math.log(0.5), math.log(2.0)))
    block_factor = jnp.exp(jax.random.uniform(key_block, (H, SEQLEN // TOK_DEV), jnp.float32, math.log(0.5), math.log(2.0)))
    return 0.1 * rough * jnp.repeat(block_factor, TOK_DEV, axis=1)


def draw_decay_rate(key, part):
    key = jax.random.fold_in(key, 23)
    key_kind, key_fast, key_slow = jax.random.split(key, 3)
    fast_share = 0.34
    quick = jax.random.uniform(key_kind, (H,), jnp.float32) < fast_share
    fast_rate = jax.random.uniform(key_fast, (H,), jnp.float32, 0.17, 0.29)
    slow_rate = jax.random.uniform(key_slow, (H,), jnp.float32, 0.2, 1.0) / (0.12 * SEQLEN)
    return jnp.where(quick, fast_rate, slow_rate)


def block_scale(stream_key, shape, cuts, low, largest):
    gain, own = 1.0, jax.random.fold_in(stream_key, 6)
    for axis_at, shards_of in cuts:
        steps = jnp.exp(jax.random.uniform(jax.random.fold_in(own, axis_at), (shards_of,), jnp.float32, low / len(cuts), largest / len(cuts)))
        gain = gain * jnp.repeat(steps, shape[axis_at] // shards_of).reshape([-1 if axis == axis_at else 1 for axis in range(len(shape))])
    return gain


def noise(key, extent, deviation, reach, pieces=(), kind=jnp.bfloat16):
    values = deviation * jax.random.normal(key, extent, jnp.float32)
    if pieces:
        values = values * block_scale(key, extent, pieces, -0.22, 0.18)
    return jnp.clip(values, -reach, reach).astype(kind)


def setup_inputs(seed: int = 0) -> dict:
    seeds = jax.random.split(jax.random.key(seed), 13)
    return {
        "queries": draw_queries(jax.random.fold_in(seeds[12], 71), 0),
        "keys": draw_keys(jax.random.fold_in(seeds[12], 71), 0),
        "values": noise(seeds[2], (SEQLEN, KVH * HD), 1.0, 6.0, ((0, 8),)),
        "length": jax.random.randint(seeds[3], (1,), SEQLEN - TOK_DEV + 1, SEQLEN + 1).astype(jnp.int32),
        "mixer_values": noise(seeds[4], (SEQLEN, XG * HD), 1.0, 6.0, ((0, 8),)),
        "mixer_keys": noise(seeds[5], (SEQLEN, XG * NST), 1.0, 6.0, ((0, 8),)),
        "mixer_queries": noise(seeds[6], (SEQLEN, H * NST), NST ** -0.5, 0.5, ((0, 8), (1, 16))),
        "gate_values": noise(seeds[7], (SEQLEN, H * HD), 1.0, 6.0, ((0, 8), (1, 16))),
        "step_size": draw_step_size(jax.random.fold_in(seeds[12], 71), 0),
        "decay_rate": draw_decay_rate(jax.random.fold_in(seeds[12], 71), 0),
        "skip_gain": jnp.clip(0.5 + 1.0 * jax.random.uniform(seeds[10], (H,), jnp.float32) ** block_scale(seeds[10], (H,), ((0, 16),), -0.2, 0.2), 0.5, 1.5),
        "out_weight": noise(seeds[11], (D, D), D ** -0.5, 0.0625, ((0, 16),)),
    }


def reference(queries, keys, values, length, mixer_values, mixer_keys, mixer_queries, gate_values, step_size, decay_rate, skip_gain, out_weight):
    positions = jnp.arange(SEQLEN, dtype=jnp.int32)
    allowed = (positions[None, :] <= positions[:, None]) & (positions[None, :] < length[0])
    group_size = H // KVH
    factor_scale = 1.0 / math.sqrt(HD)
    query_heads = queries.reshape(SEQLEN, H, HD)
    key_heads = keys.reshape(SEQLEN, KVH, HD)
    value_heads = values.reshape(SEQLEN, KVH, HD)

    def one_head(head):
        query_rows = lax.dynamic_index_in_dim(query_heads, head, 1, keepdims=False)
        key_rows = lax.dynamic_index_in_dim(key_heads, head // group_size, 1, keepdims=False)
        value_rows = lax.dynamic_index_in_dim(value_heads, head // group_size, 1, keepdims=False)
        scores = jnp.dot(query_rows, key_rows.T, preferred_element_type=jnp.float32) * factor_scale
        scores = jnp.where(allowed, scores, -jnp.inf)
        row_max = lax.optimization_barrier(jnp.max(scores, axis=1, keepdims=True))
        weights = jnp.exp(scores - row_max)
        total = lax.optimization_barrier(jnp.sum(weights, axis=1, keepdims=True))
        return jnp.dot(weights.astype(jnp.bfloat16), value_rows, preferred_element_type=jnp.float32) / total
    attended = lax.map(one_head, jnp.arange(H, dtype=jnp.int32))
    attn_heads = attended.transpose(1, 0, 2).reshape(SEQLEN, H * HD).astype(jnp.bfloat16)
    step = jnp.where(positions[None, :] < length[0], step_size, jnp.float32(0.0))
    log_decay = -step * decay_rate[:, None]
    head_group = np.arange(H) // (H // XG)
    value_groups = mixer_values.reshape(SEQLEN, XG, HD)
    key_groups = mixer_keys.reshape(SEQLEN, XG, NST)
    query_groups = mixer_queries.reshape(SEQLEN, H, NST)
    gate_groups = gate_values.reshape(SEQLEN, H, HD)
    block_pos = jnp.arange(TOK_DEV, dtype=jnp.int32)
    causal = block_pos[:, None] >= block_pos[None, :]

    def one_block(state, block):
        begin = (block * TOK_DEV).astype(jnp.int32)
        input_vals = lax.dynamic_slice_in_dim(value_groups, begin, TOK_DEV, 0)[:, head_group].astype(jnp.float32)
        input_keys = lax.dynamic_slice_in_dim(key_groups, begin, TOK_DEV, 0)[:, head_group].astype(jnp.float32)
        output_keys = lax.dynamic_slice_in_dim(query_groups, begin, TOK_DEV, 0).astype(jnp.float32)
        gate_block = lax.dynamic_slice_in_dim(gate_groups, begin, TOK_DEV, 0).astype(jnp.float32)
        step_block = lax.dynamic_slice_in_dim(step, begin, TOK_DEV, 1)
        cum = jnp.cumsum(lax.dynamic_slice_in_dim(log_decay, begin, TOK_DEV, 1), axis=1)
        inner = jnp.einsum('thn,shn->hts', output_keys, input_keys)
        diff = jnp.where(causal[None], cum[:, :, None] - cum[:, None, :], -jnp.inf)
        mix = (jnp.exp(diff) * inner * step_block[:, None, :]).astype(jnp.bfloat16)
        result = jnp.einsum('hts,shp->thp', mix.astype(jnp.float32), input_vals)
        carried = jnp.einsum('thn,hpn->thp', output_keys, state, precision=lax.Precision.HIGHEST)
        result = result + jnp.exp(cum).T[:, :, None] * carried
        result = result + skip_gain[None, :, None] * input_vals
        gated = (result * jax.nn.silu(gate_block)).astype(jnp.bfloat16)
        tail = jnp.exp(cum[:, -1:] - cum) * step_block
        weighted = input_vals * tail.T[:, :, None]
        local = jnp.einsum('shp,shn->hpn', weighted, input_keys, precision=lax.Precision.HIGHEST)
        new_state = jnp.exp(cum[:, -1])[:, None, None] * state + local
        return (new_state, gated.reshape(TOK_DEV, H * HD))
    final_states, blocks = lax.scan(one_block, jnp.zeros((H, HD, NST), jnp.float32), jnp.arange(SEQLEN // TOK_DEV, dtype=jnp.int32))
    gated_all = blocks.reshape(SEQLEN, H * HD)
    ssm_out = jnp.dot(gated_all, out_weight, preferred_element_type=jnp.float32).astype(jnp.bfloat16)
    return (attn_heads, ssm_out, final_states)
```

```python
import math

import jax
import jax.numpy as jnp
from jax import lax
from jax.experimental import pallas as pl
from jax.experimental.pallas import tpu as pltpu
from jax.sharding import PartitionSpec as P

H = 64
KVH = 8
HD = 128
NST = 128
TOK = 512
HEADS = 4
ROWS = HEADS * HD
MSG = ROWS + 32
CB = 256
BF = jnp.bfloat16
F32 = jnp.float32
NT = (((1,), (1,)), ((), ()))
VMEM_LIMIT = 48 * 1024 * 1024

SEQ, CORE, GROUP, LENGTH, YPOS, XLO, ZPOS, XHI = range(8)


def call(kernel, info, args, in_specs, out_specs, out_shape, grid=(1,), scratch=(), flops=0, nbytes=0, trans=0, alias=None, extra=()):
    spec = pltpu.PrefetchScalarGridSpec(
        num_scalar_prefetch=1 + len(extra),
        grid=grid,
        in_specs=in_specs,
        out_specs=out_specs,
        scratch_shapes=list(scratch),
    )
    return pl.pallas_call(
        kernel,
        grid_spec=spec,
        out_shape=out_shape,
        input_output_aliases=alias or {},
        compiler_params=pltpu.CompilerParams(vmem_limit_bytes=VMEM_LIMIT),
        cost_estimate=pl.CostEstimate(flops=flops, bytes_accessed=nbytes, transcendentals=trans),
    )(info, *extra, *args)


def full(shape):
    return pl.BlockSpec(shape, lambda i, *_: (0,) * len(shape))


def grouped():
    return pl.BlockSpec((TOK, HD), lambda i, info, *_: (0, info[GROUP]))


SMEM = pl.BlockSpec(memory_space=pltpu.SMEM)


def shape(dims, kind):
    return jax.ShapeDtypeStruct(dims, kind)


def split2(a):
    high = a.astype(BF)
    return high, (a - high.astype(F32)).astype(BF)


def prep_kernel(info, k_ref, v_ref, mv_ref, mk_ref, step_ref, rate_ref, kv_ref, msg_ref, cum_ref):
    @pl.when(info[CORE] == 0)
    def _():
        kv_ref[...] = k_ref[...]

    @pl.when(info[CORE] == 1)
    def _():
        for i in range(TOK // HD):
            part = pl.ds(i * HD, HD)
            kv_ref[part, :] = v_ref[part, :].astype(F32).T.astype(BF)

    row = lax.broadcasted_iota(jnp.int32, (8, TOK), 0)
    lane = lax.broadcasted_iota(jnp.int32, (8, TOK), 1)
    step = jnp.concatenate([step_ref[...], jnp.zeros((8 - HEADS, TOK), F32)], axis=0)
    step = jnp.where(info[SEQ] * TOK + lane < info[LENGTH], step, 0.0)
    rate = jnp.zeros((8, TOK), F32)
    for h in range(HEADS):
        rate = jnp.where(row == h, rate_ref[h], rate)
    cum = -step * rate
    shift = 1
    while shift < TOK:
        cum = cum + jnp.where(lane >= shift, pltpu.roll(cum, shift, 1), 0.0)
        shift *= 2
    cum_ref[0:8, :] = cum
    cum_ref[8:16, :] = step
    last = cum[:, TOK - 1 : TOK]
    tail = jnp.exp(last - cum) * step
    log = jnp.broadcast_to(last, (8, HD))
    high = log.astype(BF).astype(F32)
    mid = (log - high).astype(BF).astype(F32)
    low = log - high - mid
    msg_ref[ROWS:MSG, :] = jnp.concatenate([high, mid, low, jnp.zeros_like(low)], axis=0).astype(BF)
    vt = mv_ref[...].astype(F32).T
    mk = mk_ref[...]
    for h in range(HEADS):
        high, low = split2(vt * tail[h : h + 1, :])
        state = jnp.dot(high, mk, preferred_element_type=F32) + jnp.dot(low, mk, preferred_element_type=F32)
        msg_ref[h * HD : (h + 1) * HD, :] = state.astype(BF)


def log_of(msg):
    tail = msg[ROWS:MSG, :].astype(F32)
    return tail[0:8] + tail[8:16] + tail[16:24]


def combine_kernel(info, m0, m1, m2, m3, prefix_ref, pdec_ref, total_ref):
    y = info[YPOS]
    msgs = (m0, m1, m2, m3)
    place = [lax.rem(y - d + 4, 4) for d in range(4)]
    logs = [log_of(m) for m in msgs]
    pre, tot = [], []
    for d in range(4):
        in_pre = jnp.zeros_like(logs[0])
        in_tot = jnp.zeros_like(logs[0])
        for e in range(4):
            if e == d:
                continue
            after = place[e] > place[d]
            in_tot = in_tot + jnp.where(after, logs[e], 0.0)
            in_pre = in_pre + jnp.where(jnp.logical_and(after, place[e] < y), logs[e], 0.0)
        tot.append(jnp.exp(in_tot))
        pre.append(jnp.where(place[d] < y, jnp.exp(in_pre), 0.0))
    whole = logs[0] + logs[1] + logs[2] + logs[3]
    before = jnp.zeros_like(whole)
    for e in range(4):
        before = before + jnp.where(place[e] < y, logs[e], 0.0)
    pdec_ref[...] = jnp.exp(before)
    for h in range(HEADS):
        part = slice(h * HD, (h + 1) * HD)
        own = [m[part, :].astype(F32) for m in msgs]
        total = own[0] * tot[0][h : h + 1]
        prefix = own[1] * pre[1][h : h + 1]
        for d in range(1, 4):
            total = total + own[d] * tot[d][h : h + 1]
        for d in range(2, 4):
            prefix = prefix + own[d] * pre[d][h : h + 1]
        prefix_ref[part, :] = prefix
        total_ref[part, :] = total.astype(BF)
    high = whole.astype(BF).astype(F32)
    mid = (whole - high).astype(BF).astype(F32)
    low = whole - high - mid
    total_ref[ROWS:MSG, :] = jnp.concatenate([high, mid, low, jnp.zeros_like(low)], axis=0).astype(BF)


def intra_kernel(info, cum_ref, c_ref, mk_ref, mv_ref, skip_ref, y_ref):
    cum = cum_ref[0:8, :]
    step = cum_ref[8:16, :]
    cols = cum.T
    half = TOK // 2
    for h in range(HEADS):
        part = slice(h * HD, (h + 1) * HD)
        for i in range(2):
            here = slice(i * half, (i + 1) * half)
            wide = (i + 1) * half
            inner = lax.dot_general(c_ref[here, part], mk_ref[0:wide, :], NT, preferred_element_type=F32)
            t = i * half + lax.broadcasted_iota(jnp.int32, (half, wide), 0)
            s = lax.broadcasted_iota(jnp.int32, (half, wide), 1)
            diff = jnp.where(s <= t, cols[here, h : h + 1] - cum[h : h + 1, 0:wide], -jnp.inf)
            mix = (jnp.exp(diff) * inner * step[h : h + 1, 0:wide]).astype(BF)
            y = jnp.dot(mix, mv_ref[0:wide, :], preferred_element_type=F32)
            y_ref[here, part] = y + skip_ref[h] * mv_ref[here, :].astype(F32)


def gate_kernel(info, cum_ref, c_ref, y_ref, g_ref, prefix_ref, pdec_ref, own_ref, got_ref, out_ref, fin_ref):
    second = info[XLO] == 1
    ecols = jnp.exp(cum_ref[0:8, :]).T
    for h in range(HEADS):
        part = slice(h * HD, (h + 1) * HD)
        far = pdec_ref[h : h + 1, :] * got_ref[part, :].astype(F32)
        state = prefix_ref[part, :] + jnp.where(second, far, 0.0)
        high, low = split2(state)
        c = c_ref[:, part]
        carried = lax.dot_general(
            jnp.concatenate([c, c], axis=1), jnp.concatenate([high, low], axis=1), NT, preferred_element_type=F32
        )
        y = y_ref[:, part] + ecols[:, h : h + 1] * carried
        g = g_ref[:, part].astype(F32)
        out_ref[:, part] = (y * (g / (1.0 + jnp.exp(-g)))).astype(BF)
    own_log = log_of(own_ref)
    got_log = log_of(got_ref)
    later = jnp.exp(jnp.where(second, own_log, got_log))
    for h in range(HEADS):
        rows = pl.ds(pl.multiple_of(h * HD + info[SEQ] * (HD // 8), HD // 8), HD // 8)
        own = own_ref[rows, :].astype(F32)
        got = got_ref[rows, :].astype(F32)
        first = jnp.where(second, got, own)
        last = jnp.where(second, own, got)
        fin_ref[h] = last + later[h : h + 1, :] * first


def place_kernel(info, *refs):
    mine, other, (k_ref, v_ref) = refs[0:5], refs[5:10], refs[10:12]
    zero = info[CORE] == 0
    y, x = info[YPOS], info[XLO]

    def put(a, b, where):
        rows = pl.ds(pl.multiple_of(where * TOK, TOK), TOK)
        a, b = a.astype(F32), b.astype(F32)
        k_ref[rows, :] = jnp.where(zero, a, b).astype(BF)
        v_ref[rows, :] = jnp.where(zero, b, a).astype(BF)

    put(mine[0][...], other[0][...], x * 4 + y)
    put(mine[1][...], other[1][...], (1 - x) * 4 + y)
    for d in range(1, 4):
        ypos = lax.rem(y - d + 4, 4)
        put(mine[d + 1][0:TOK, :], other[d + 1][0:TOK, :], x * 4 + ypos)
        put(mine[d + 1][TOK : 2 * TOK, :], other[d + 1][TOK : 2 * TOK, :], (1 - x) * 4 + ypos)


def attend_kernel(info, q_ref, k_ref, v_ref, *rest):
    out_ref = rest[-1]
    seq = info[SEQ]
    scale = math.log2(math.e) / math.sqrt(HD)
    half = TOK // 2
    queries = [q_ref[i * half : (i + 1) * half, :] for i in range(2)]
    ones = jnp.ones((16, TOK), BF)

    def tile(j):
        base = pl.multiple_of(j * TOK, TOK)
        k = k_ref[pl.ds(base, TOK), :]
        vt = jnp.concatenate([v_ref[pl.ds(base + i * HD, HD), :] for i in range(TOK // HD)], axis=1)
        return k, jnp.concatenate([vt, ones], axis=0)

    k, vt = tile(seq)
    state = []
    for i in range(2):
        wide = (i + 1) * half
        scores = lax.dot_general(k[0:wide], queries[i], NT, preferred_element_type=F32)
        s = lax.broadcasted_iota(jnp.int32, (wide, half), 0)
        t = i * half + lax.broadcasted_iota(jnp.int32, (wide, half), 1)
        keep = jnp.logical_and(s <= t, s < info[LENGTH] - seq * TOK)
        scores = jnp.where(keep, scores, -jnp.inf)
        best = jnp.max(scores, axis=0, keepdims=True)
        weights = jnp.exp2((scores - best) * scale).astype(BF)
        state += [best, jnp.dot(vt[:, 0:wide], weights, preferred_element_type=F32)]

    def one(j, state):
        k, vt = tile(j)
        new = []
        for i in range(2):
            best, summed = state[2 * i], state[2 * i + 1]
            scores = lax.dot_general(k, queries[i], NT, preferred_element_type=F32)
            top = jnp.maximum(best, jnp.max(scores, axis=0, keepdims=True))
            weights = jnp.exp2((scores - top) * scale).astype(BF)
            shrink = jnp.exp2((best - top) * scale)
            new += [top, summed * shrink + jnp.dot(vt, weights, preferred_element_type=F32)]
        return tuple(new)

    state = lax.fori_loop(0, seq, one, tuple(state))
    for i in range(2):
        summed = state[2 * i + 1]
        out = summed[0:HD] * (1.0 / summed[HD : HD + 1])
        out_ref[i * half : (i + 1) * half, :] = out.T.astype(BF)


def project_kernel(n_got, info, columns, *refs):
    g0, g1, w0, w1 = refs[0:4]
    got, out_ref = refs[4 : 4 + n_got], refs[4 + n_got]
    acc = jnp.dot(g0[...], w0[...], preferred_element_type=F32) + jnp.dot(
        g1[...], w1[...], preferred_element_type=F32
    )
    for r in got:
        acc = acc + r[...].reshape(TOK, CB).astype(F32)
    out_ref[...] = acc.astype(BF).reshape(out_ref.shape)


def project(info, operands, columns, got=(), got_specs=()):
    n = columns.shape[0]
    weight = pl.BlockSpec((TOK, CB), lambda i, info, columns: (0, columns[i]))
    return call(
        lambda *refs: project_kernel(len(got), *refs),
        info,
        (*operands, *got),
        [full((TOK, TOK)), full((TOK, TOK)), weight, weight, *got_specs],
        pl.BlockSpec((1, TOK, CB), lambda i, *_: (i, 0, 0)),
        shape((n, TOK, CB), BF),
        grid=(n,),
        flops=2 * n * TOK * 1024 * CB,
        nbytes=n * 1024 * CB * 2 + 2**20,
        extra=(columns,),
    )


def finish_kernel(info, columns, g0, g1, w0, w1, a1, a2, a3, ax, b1, b2, b3, bx, out_ref):
    acc = jnp.dot(g0[...], w0[...], preferred_element_type=F32) + jnp.dot(
        g1[...], w1[...], preferred_element_type=F32
    )

    @pl.when(pl.program_id(0) == 0)
    def _():
        total = acc
        for r in (a1, a2, a3):
            total = total + r[0].astype(F32)
        out_ref[...] = (total + ax[0].astype(F32)).astype(BF)

    @pl.when(pl.program_id(0) == 1)
    def _():
        total = acc + bx[0].astype(F32)
        for r in (b1, b2, b3):
            total = total + r[0].astype(F32)
        out_ref[...] = total.astype(BF)


def head_perm(move):
    pairs = []
    for z in range(4):
        for x in range(2):
            for c in range(2):
                z2, x2, c2 = move(z, x, c)
                pairs.append((z * 4 + x * 2 + c, (z2 % 4) * 4 + (x2 % 2) * 2 + c2 % 2))
    return pairs


CORE_SWAP = head_perm(lambda z, x, c: (z, x, c + 1))
X_SWAP = head_perm(lambda z, x, c: (z, x + 1, c))
Z_MOVE = {d: head_perm(lambda z, x, c, d=d: (z + d, x, c)) for d in (1, 2, 3)}
LO_SWAP = [(i, (i + 4) % 8) for i in range(8)]
Y_MOVE = {d: [(x * 4 + y, x * 4 + (y + d) % 4) for x in range(2) for y in range(4)] for d in (1, 2, 3)}


def body(
    queries,
    keys,
    values,
    length,
    mixer_values,
    mixer_keys,
    mixer_queries,
    gate_values,
    step_size,
    decay_rate,
    skip_gain,
    out_weight,
):
    seq = lax.axis_index("seq")
    head = lax.axis_index("head")
    z, x, c = head // 4, (head // 2) % 2, head % 2
    info = jnp.stack([seq, c, head // 2, length[0], seq % 4, seq // 4, z, x]).astype(jnp.int32)
    core = lambda a: lax.ppermute(a, "head", CORE_SWAP)
    lo = lambda a: lax.ppermute(a, "seq", LO_SWAP)
    along_y = lambda a, d: lax.ppermute(a, "seq", Y_MOVE[d])
    along_z = lambda a, d: lax.ppermute(a, "head", Z_MOVE[d])

    far_weight = core(out_weight)

    kv, msg, cum = call(
        prep_kernel,
        info,
        (keys, values, mixer_values, mixer_keys, step_size, decay_rate),
        [grouped(), grouped(), grouped(), grouped(), full((HEADS, TOK)), SMEM],
        [full((TOK, HD)), full((MSG, HD)), full((16, TOK))],
        [shape((TOK, HD), BF), shape((MSG, HD), BF), shape((16, TOK), F32)],
        flops=2 * 2 * TOK * TOK * HD,
        nbytes=2**20,
    )
    msgs = [msg] + [along_y(msg, d) for d in (1, 2, 3)]
    kv_far = lo(kv)

    y_in = call(
        intra_kernel,
        info,
        (cum, mixer_queries, mixer_keys, mixer_values, skip_gain),
        [full((16, TOK)), full((TOK, ROWS)), grouped(), grouped(), SMEM],
        full((TOK, ROWS)),
        shape((TOK, ROWS), F32),
        flops=4 * 2 * 2 * TOK * TOK * HD,
        nbytes=2**21,
        trans=4 * TOK * TOK,
    )
    prefix, pdec, total = call(
        combine_kernel,
        info,
        msgs,
        [full((MSG, HD))] * 4,
        [full((ROWS, HD)), full((8, HD)), full((MSG, HD))],
        [shape((ROWS, HD), F32), shape((8, HD), F32), shape((MSG, HD), BF)],
        flops=2**20,
        nbytes=2**20,
    )
    total_far = lo(total)
    gated, final_states = call(
        gate_kernel,
        info,
        (cum, mixer_queries, y_in, gate_values, prefix, pdec, total, total_far),
        [
            full((16, TOK)),
            full((TOK, ROWS)),
            full((TOK, ROWS)),
            full((TOK, ROWS)),
            full((ROWS, HD)),
            full((8, HD)),
            full((MSG, HD)),
            full((MSG, HD)),
        ],
        [full((TOK, ROWS)), full((HEADS, HD // 8, NST))],
        [shape((TOK, ROWS), BF), shape((HEADS, HD // 8, NST), F32)],
        flops=4 * 2 * TOK * 256 * HD,
        nbytes=2**21,
    )
    far_gated = core(gated)

    kv_pair = jnp.concatenate([kv, kv_far], axis=0)
    mine = [kv, kv_far] + [along_y(kv_pair, d) for d in (1, 2, 3)]
    other = [core(a) for a in mine]
    pieces = [full((TOK, HD))] * 2 + [full((2 * TOK, HD))] * 3
    k_all, v_all = call(
        place_kernel,
        info,
        (*mine, *other),
        pieces * 2,
        [full((8 * TOK, HD))] * 2,
        [shape((8 * TOK, HD), BF)] * 2,
        flops=2**20,
        nbytes=2**22,
    )
    attended = None
    for h in range(HEADS):
        column = pl.BlockSpec((TOK, HD), lambda i, info, h=h: (0, h))
        prior = () if attended is None else (attended,)
        attended = call(
            attend_kernel,
            info,
            (queries, k_all, v_all, *prior),
            [column, full((8 * TOK, HD)), full((8 * TOK, HD))] + [pl.BlockSpec(memory_space=pl.ANY)] * len(prior),
            column,
            shape((TOK, ROWS), BF),
            flops=2 * 2 * TOK * HD * TOK * 8,
            nbytes=2**21,
            trans=8 * TOK * TOK,
            alias={4: 0} if prior else None,
        )

    operands = (gated, far_gated, out_weight, far_weight)
    block = lambda zz, xx, half: ((zz % 4) * 4 + (xx % 2) * 2 + c) * 2 + half
    cols = lambda items: jnp.stack(items).astype(jnp.int32)

    to_x = project(info, operands, cols([block(i, x + 1, 1) for i in range(4)]))
    from_x = lax.ppermute(to_x, "head", X_SWAP)
    from_z = {}
    for d in (2, 1, 3):
        to_z = project(info, operands, cols([block(z + d, i, 0) for i in range(2)]))
        from_z[d] = along_z(to_z, d)

    arrived = [from_z[d] for d in (1, 2, 3)]
    turned = pl.BlockSpec((1, TOK, CB), lambda i, info, columns: (1 - info[XHI], 0, 0))
    to_x2 = project(info, operands, cols([block(z, x + 1, 0)]), arrived, [turned] * 3)
    from_x2 = lax.ppermute(to_x2, "head", X_SWAP)
    from_z2 = {}
    for d in (2, 1, 3):
        row = pl.BlockSpec((1, TOK, CB), lambda i, info, columns, d=d: (lax.rem(info[ZPOS] + d, 4), 0, 0))
        to_z2 = project(info, operands, cols([block(z + d, x, 1)]), [from_x], [row])
        from_z2[d] = along_z(to_z2, d)

    own_x = pl.BlockSpec((1, TOK, CB), lambda i, info, columns: (info[XHI], 0, 0))
    own_z = pl.BlockSpec((1, TOK, CB), lambda i, info, columns: (info[ZPOS], 0, 0))
    one = full((1, TOK, CB))
    weight = pl.BlockSpec((TOK, CB), lambda i, info, columns: (0, columns[i]))
    summed = call(
        finish_kernel,
        info,
        (*operands, *arrived, from_x2, from_z2[1], from_z2[2], from_z2[3], from_x),
        [full((TOK, TOK)), full((TOK, TOK)), weight, weight, own_x, own_x, own_x, one, one, one, one, own_z],
        pl.BlockSpec((TOK, CB), lambda i, *_: (0, i)),
        shape((TOK, ROWS), BF),
        grid=(2,),
        flops=2 * 2 * TOK * 1024 * CB,
        nbytes=2**22,
        extra=(cols([block(z, x, 0), block(z, x, 1)]),),
    )
    return (attended, summed, final_states)


def solution(mesh):
    placed = (
        P("seq", "head"),
        P("seq", None),
        P("seq", None),
        P(),
        P("seq", None),
        P("seq", None),
        P("seq", "head"),
        P("seq", "head"),
        P("head", "seq"),
        P("head"),
        P("head"),
        P("head", None),
    )
    return jax.shard_map(
        body,
        mesh=mesh,
        in_specs=placed,
        out_specs=(P("seq", "head"), P("seq", "head"), P("head", "seq", None)),
        check_vma=False,
    )
```

```python
import math

import jax
import jax.numpy as jnp
from jax import lax
from jax.experimental import pallas as pl
from jax.experimental.pallas import tpu as pltpu
from jax.sharding import PartitionSpec as P

H = 64
KVH = 8
HD = 128
NST = 128
TOK = 512
HEADS = 4
ROWS = HEADS * HD
MSG = ROWS + 32
CB = 256
BF = jnp.bfloat16
F32 = jnp.float32
US = 10**5
NT = (((1,), (1,)), ((), ()))
VMEM_LIMIT = 28 * 1024 * 1024

SEQ, CORE, GROUP, LENGTH, YPOS, XLO, ZPOS, XHI = range(8)


def call(kernel, info, args, in_specs, out_specs, out_shape, grid=(1,), scratch=(), flops=0, nbytes=0, trans=0, extra=(), after=(), limit=VMEM_LIMIT, alias=None):
    scalars = 1 + len(extra)
    first = scalars + len(args)

    def run(*refs):
        kernel(*refs[:first], *refs[first + len(after) :])

    aliases = {} if alias is None else {first + alias: 0}

    spec = pltpu.PrefetchScalarGridSpec(
        num_scalar_prefetch=scalars,
        grid=grid,
        in_specs=[*in_specs, *[ANY] * len(after)],
        out_specs=out_specs,
        scratch_shapes=list(scratch),
    )
    return pl.pallas_call(
        run,
        grid_spec=spec,
        out_shape=out_shape,
        input_output_aliases=aliases,
        compiler_params=pltpu.CompilerParams(vmem_limit_bytes=limit),
        cost_estimate=pl.CostEstimate(flops=flops, bytes_accessed=nbytes, transcendentals=trans),
    )(info, *extra, *args, *after)


def full(shape):
    return pl.BlockSpec(shape, lambda i, *_: (0,) * len(shape))


def hbm(a):
    return pltpu.with_memory_space_constraint(a, pltpu.HBM)


ANY = pl.BlockSpec(memory_space=pl.ANY)
HBM = pl.BlockSpec(memory_space=pltpu.HBM)
VMEM = pl.BlockSpec(memory_space=pltpu.VMEM)
SMEM = pl.BlockSpec(memory_space=pltpu.SMEM)


def shape(dims, kind):
    return jax.ShapeDtypeStruct(dims, kind)


def split2(a):
    high = a.astype(BF)
    return high, (a - high.astype(F32)).astype(BF)


def prep_kernel(
    info, k_hbm, v_hbm, mv_hbm, mk_hbm, step_ref, rate_ref, k_ref, vt_ref, kv_ref, msg_ref, cum_ref, mv_ref, mk_ref, v_ref, sems
):
    columns = pl.ds(pl.multiple_of(info[GROUP] * HD, HD), HD)
    pairs = ((mv_hbm, mv_ref), (mk_hbm, mk_ref), (k_hbm, k_ref), (v_hbm, v_ref))
    copies = [pltpu.make_async_copy(a.at[:, columns], b, sems.at[i]) for i, (a, b) in enumerate(pairs)]
    for copy in copies:
        copy.start()

    row = lax.broadcasted_iota(jnp.int32, (8, TOK), 0)
    lane = lax.broadcasted_iota(jnp.int32, (8, TOK), 1)
    step = jnp.concatenate([step_ref[...], jnp.zeros((8 - HEADS, TOK), F32)], axis=0)
    step = jnp.where(info[SEQ] * TOK + lane < info[LENGTH], step, 0.0)
    rate = jnp.zeros((8, TOK), F32)
    for h in range(HEADS):
        rate = jnp.where(row == h, rate_ref[h], rate)
    cum = -step * rate
    shift = 1
    while shift < TOK:
        cum = cum + jnp.where(lane >= shift, pltpu.roll(cum, shift, 1), 0.0)
        shift *= 2
    cum_ref[0:8, :] = cum
    cum_ref[8:16, :] = step
    last = cum[:, TOK - 1 : TOK]
    tail = jnp.exp(last - cum) * step
    log = jnp.broadcast_to(last, (8, HD))
    high = log.astype(BF).astype(F32)
    mid = (log - high).astype(BF).astype(F32)
    low = log - high - mid
    msg_ref[ROWS:MSG, :] = jnp.concatenate([high, mid, low, jnp.zeros_like(low)], axis=0).astype(BF)
    copies[0].wait()
    copies[1].wait()
    vt = mv_ref[...].astype(F32).T
    mk = mk_ref[...]
    for h in range(HEADS):
        high, low = split2(vt * tail[h : h + 1, :])
        state = jnp.dot(high, mk, preferred_element_type=F32) + jnp.dot(low, mk, preferred_element_type=F32)
        msg_ref[h * HD : (h + 1) * HD, :] = state.astype(BF)
    copies[2].wait()
    copies[3].wait()
    zero = info[CORE] == 0
    for i in range(TOK // HD):
        part = pl.ds(i * HD, HD)
        turned = v_ref[part, :].astype(F32).T
        vt_ref[part, :] = turned.astype(BF)
        kv_ref[part, :] = jnp.where(zero, k_ref[part, :].astype(F32), turned).astype(BF)


def log_of(msg):
    tail = msg[ROWS:MSG, :].astype(F32)
    return tail[0:8] + tail[8:16] + tail[16:24]


def combine_kernel(info, m0, m1, m2, m3, kv, kv_far, prefix_ref, pdec_ref, total_ref, pair_ref):
    pair_ref[0:TOK, :] = kv[...]
    pair_ref[TOK : 2 * TOK, :] = kv_far[...]
    y = info[YPOS]
    msgs = (m0, m1, m2, m3)
    place = [lax.rem(y - d + 4, 4) for d in range(4)]
    logs = [log_of(m) for m in msgs]
    pre, tot = [], []
    for d in range(4):
        in_pre = jnp.zeros_like(logs[0])
        in_tot = jnp.zeros_like(logs[0])
        for e in range(4):
            if e == d:
                continue
            after = place[e] > place[d]
            in_tot = in_tot + jnp.where(after, logs[e], 0.0)
            in_pre = in_pre + jnp.where(jnp.logical_and(after, place[e] < y), logs[e], 0.0)
        tot.append(jnp.exp(in_tot))
        pre.append(jnp.where(place[d] < y, jnp.exp(in_pre), 0.0))
    whole = logs[0] + logs[1] + logs[2] + logs[3]
    before = jnp.zeros_like(whole)
    for e in range(4):
        before = before + jnp.where(place[e] < y, logs[e], 0.0)
    pdec_ref[...] = jnp.exp(before)
    for h in range(HEADS):
        part = slice(h * HD, (h + 1) * HD)
        own = [m[part, :].astype(F32) for m in msgs]
        total = own[0] * tot[0][h : h + 1]
        prefix = own[1] * pre[1][h : h + 1]
        for d in range(1, 4):
            total = total + own[d] * tot[d][h : h + 1]
        for d in range(2, 4):
            prefix = prefix + own[d] * pre[d][h : h + 1]
        prefix_ref[part, :] = prefix
        total_ref[part, :] = total.astype(BF)
    high = whole.astype(BF).astype(F32)
    mid = (whole - high).astype(BF).astype(F32)
    low = whole - high - mid
    total_ref[ROWS:MSG, :] = jnp.concatenate([high, mid, low, jnp.zeros_like(low)], axis=0).astype(BF)


def intra_kernel(info, cum_ref, c_ref, mk_ref, mv_ref, skip_ref, y_ref):
    cum = cum_ref[0:8, :]
    step = cum_ref[8:16, :]
    cols = cum.T
    half = TOK // 2
    for h in range(HEADS):
        part = slice(h * HD, (h + 1) * HD)
        for i in range(2):
            here = slice(i * half, (i + 1) * half)
            wide = (i + 1) * half
            inner = lax.dot_general(c_ref[here, part], mk_ref[0:wide, :], NT, preferred_element_type=F32)
            t = i * half + lax.broadcasted_iota(jnp.int32, (half, wide), 0)
            s = lax.broadcasted_iota(jnp.int32, (half, wide), 1)
            diff = jnp.where(s <= t, cols[here, h : h + 1] - cum[h : h + 1, 0:wide], -jnp.inf)
            mix = (jnp.exp(diff) * inner * step[h : h + 1, 0:wide]).astype(BF)
            y = jnp.dot(mix, mv_ref[0:wide, :], preferred_element_type=F32)
            y_ref[here, part] = y + skip_ref[h] * mv_ref[here, :].astype(F32)


def gate_kernel(info, cum_ref, c_ref, y_ref, g_ref, prefix_ref, pdec_ref, own_ref, got_ref, out0, out1, out2, out3, fin_ref):
    second = info[XLO] == 1
    ecols = jnp.exp(cum_ref[0:8, :]).T
    for h in range(HEADS):
        part = slice(h * HD, (h + 1) * HD)
        far = pdec_ref[h : h + 1, :] * got_ref[part, :].astype(F32)
        state = prefix_ref[part, :] + jnp.where(second, far, 0.0)
        high, low = split2(state)
        c = c_ref[:, part]
        carried = lax.dot_general(
            jnp.concatenate([c, c], axis=1), jnp.concatenate([high, low], axis=1), NT, preferred_element_type=F32
        )
        y = y_ref[:, part] + ecols[:, h : h + 1] * carried
        g = g_ref[:, part].astype(F32)
        (out0, out1, out2, out3)[h][...] = (y * (g / (1.0 + jnp.exp(-g)))).astype(BF)
    own_log = log_of(own_ref)
    got_log = log_of(got_ref)
    later = jnp.exp(jnp.where(second, own_log, got_log))
    for h in range(HEADS):
        rows = pl.ds(pl.multiple_of(h * HD + info[SEQ] * (HD // 8), HD // 8), HD // 8)
        own = own_ref[rows, :].astype(F32)
        got = got_ref[rows, :].astype(F32)
        first = jnp.where(second, got, own)
        last = jnp.where(second, own, got)
        fin_ref[h] = last + later[h : h + 1, :] * first


def place_kernel(info, *refs):
    mine, other, (k_ref, v_ref) = refs[0:5], refs[5:10], refs[10:12]
    zero = info[CORE] == 0
    y, x = info[YPOS], info[XLO]

    def put(a, b, where):
        rows = pl.ds(pl.multiple_of(where * TOK, TOK), TOK)
        a, b = a.astype(F32), b.astype(F32)
        k_ref[rows, :] = jnp.where(zero, a, b).astype(BF)
        v_ref[rows, :] = jnp.where(zero, b, a).astype(BF)

    put(mine[0][...], other[0][...], x * 4 + y)
    put(mine[1][...], other[1][...], (1 - x) * 4 + y)
    for d in range(1, 4):
        ypos = lax.rem(y - d + 4, 4)
        put(mine[d + 1][0:TOK, :], other[d + 1][0:TOK, :], x * 4 + ypos)
        put(mine[d + 1][TOK : 2 * TOK, :], other[d + 1][TOK : 2 * TOK, :], (1 - x) * 4 + ypos)


SCALE = math.log2(math.e) / math.sqrt(HD)
HALF = TOK // 2
UNITS = [(h, i) for h in range(HEADS) for i in range(2)]
ACC = HD + 16


def with_ones(panels):
    vt = jnp.concatenate(panels, axis=1)
    return jnp.concatenate([vt, jnp.ones((16, vt.shape[1]), BF)], axis=0)


def diagonal_kernel(info, q_ref, k_ref, v_ref, best_ref, acc_ref):
    limit = info[LENGTH] - info[SEQ] * TOK
    vt = with_ones([v_ref[i * HD : (i + 1) * HD, :] for i in range(TOK // HD)])
    for u, (h, i) in enumerate(UNITS):
        wide = (i + 1) * HALF
        q = q_ref[i * HALF : (i + 1) * HALF, h * HD : (h + 1) * HD]
        scores = lax.dot_general(k_ref[0:wide, :], q, NT, preferred_element_type=F32)
        s = lax.broadcasted_iota(jnp.int32, (wide, HALF), 0)
        t = i * HALF + lax.broadcasted_iota(jnp.int32, (wide, HALF), 1)
        keep = jnp.logical_and(s <= t, s < limit)
        scores = jnp.where(keep, scores, -jnp.inf)
        best = jnp.max(scores, axis=0, keepdims=True)
        weights = jnp.exp2((scores - best) * SCALE).astype(BF)
        best_ref[u] = jnp.broadcast_to(best, (8, HALF))
        acc_ref[u] = jnp.dot(vt[:, 0:wide], weights, preferred_element_type=F32)


def earlier_kernel(heads, info, q_ref, k_ref, v_ref, best_ref, acc_ref, out_ref):
    units = [(h, i) for h in range(heads) for i in range(2)]
    queries = [q_ref[i * HALF : (i + 1) * HALF, h * HD : (h + 1) * HD] for h, i in units]

    def one(j, state):
        base = pl.multiple_of(j * TOK, TOK)
        k = k_ref[pl.ds(base, TOK), :]
        vt = with_ones([v_ref[pl.ds(base + i * HD, HD), :] for i in range(TOK // HD)])
        scores = [lax.dot_general(k, q, NT, preferred_element_type=F32) for q in queries]
        new = []
        for u in range(len(units)):
            best, summed = state[2 * u], state[2 * u + 1]
            top = jnp.maximum(best, jnp.max(scores[u], axis=0, keepdims=True))
            weights = jnp.exp2((scores[u] - top) * SCALE).astype(BF)
            shrink = jnp.exp2((best - top) * SCALE)
            new += [top, summed * shrink + jnp.dot(vt, weights, preferred_element_type=F32)]
        return tuple(new)

    start = []
    for u in range(len(units)):
        start += [best_ref[u, 0:1, :], acc_ref[u]]
    state = lax.fori_loop(0, info[SEQ], one, tuple(start))
    for u, (h, i) in enumerate(units):
        summed = state[2 * u + 1]
        out = summed[0:HD] * (1.0 / summed[HD : HD + 1])
        out_ref[i * HALF : (i + 1) * HALF, h * HD : (h + 1) * HD] = out.T.astype(BF)


def weights_kernel(info, columns, near, far, out_ref, sems):
    def copies(k):
        part = pl.ds(pl.multiple_of(columns[k] * CB, CB), CB)
        return (
            pltpu.make_async_copy(near.at[:, part], out_ref.at[k, 0:TOK, :], sems.at[0, k]),
            pltpu.make_async_copy(far.at[:, part], out_ref.at[k, TOK : 2 * TOK, :], sems.at[1, k]),
        )

    for k in range(16):
        for copy in copies(k):
            copy.start()
    for k in range(16):
        for copy in copies(k):
            copy.wait()


def product(gated, weights, first, n):
    g = jnp.concatenate([r[...] for r in gated], axis=1)
    w = jnp.concatenate([weights[first + k] for k in range(n)], axis=1)
    return jnp.dot(g, w, preferred_element_type=F32)


def first_kernel(info, *refs):
    gated, weights, to_x, to_z = refs[0:8], refs[8], refs[9], refs[10:13]
    for i in range(2):
        acc = product(gated, weights, 2 * i, 2).astype(BF)
        to_x[2 * i] = acc[:, 0:CB]
        to_x[2 * i + 1] = acc[:, CB : 2 * CB]
    for d in range(3):
        acc = product(gated, weights, 4 + 2 * d, 2).astype(BF)
        to_z[d][0] = acc[:, 0:CB]
        to_z[d][1] = acc[:, CB : 2 * CB]


def second_kernel(info, *refs):
    gated, (weights, z1, z2, z3, x, to_x), to_z = refs[0:8], refs[8:14], refs[14:17]
    acc = product(gated, weights, 10, 2)
    total = acc[:, 0:CB]
    for r in (z1, z2, z3):
        total = total + r[1 - info[XHI]].astype(F32)
    to_x[...] = total.astype(BF)
    part = acc[:, CB : 2 * CB]
    to_z[0][...] = (part + x[lax.rem(info[ZPOS] + 1, 4)].astype(F32)).astype(BF)
    acc = product(gated, weights, 12, 2)
    for d in (1, 2):
        part = acc[:, (d - 1) * CB : d * CB]
        to_z[d][...] = (part + x[lax.rem(info[ZPOS] + d + 1, 4)].astype(F32)).astype(BF)


def keep_kernel(info, *refs):
    gated, (weights, z1, z2, z3, x, out_ref) = refs[0:8], refs[8:14]
    acc = product(gated, weights, 14, 2)
    total = acc[:, 0:CB]
    for r in (z1, z2, z3):
        total = total + r[info[XHI]].astype(F32)
    out_ref[:, 0:CB] = total
    out_ref[:, CB : 2 * CB] = acc[:, CB : 2 * CB] + x[info[ZPOS]].astype(F32)


def finish_kernel(info, kept, x, z1, z2, z3, out_ref):
    out_ref[:, 0:CB] = (kept[:, 0:CB] + x[...].astype(F32)).astype(BF)
    total = kept[:, CB : 2 * CB]
    for r in (z1, z2, z3):
        total = total + r[...].astype(F32)
    out_ref[:, CB : 2 * CB] = total.astype(BF)


def head_perm(move):
    pairs = []
    for z in range(4):
        for x in range(2):
            for c in range(2):
                z2, x2, c2 = move(z, x, c)
                pairs.append((z * 4 + x * 2 + c, (z2 % 4) * 4 + (x2 % 2) * 2 + c2 % 2))
    return pairs


CORE_SWAP = head_perm(lambda z, x, c: (z, x, c + 1))
X_SWAP = head_perm(lambda z, x, c: (z, x + 1, c))
Z_MOVE = {d: head_perm(lambda z, x, c, d=d: (z + d, x, c)) for d in (1, 2, 3)}
LO_SWAP = [(i, (i + 4) % 8) for i in range(8)]
Y_MOVE = {d: [(x * 4 + y, x * 4 + (y + d) % 4) for x in range(2) for y in range(4)] for d in (1, 2, 3)}


def body(
    queries,
    keys,
    values,
    length,
    mixer_values,
    mixer_keys,
    mixer_queries,
    gate_values,
    step_size,
    decay_rate,
    skip_gain,
    out_weight,
):
    seq = lax.axis_index("seq")
    head = lax.axis_index("head")
    z, x, c = head // 4, (head // 2) % 2, head % 2
    info = jnp.stack([seq, c, head // 2, length[0], seq % 4, seq // 4, z, x]).astype(jnp.int32)
    core = lambda a: lax.ppermute(a, "head", CORE_SWAP)
    lo = lambda a: lax.ppermute(a, "seq", LO_SWAP)
    along_y = lambda a, d: lax.ppermute(a, "seq", Y_MOVE[d])
    along_z = lambda a, d: lax.ppermute(a, "head", Z_MOVE[d])

    far_weight = core(out_weight)
    keys, values, mixer_values, mixer_keys = hbm(keys), hbm(values), hbm(mixer_values), hbm(mixer_keys)
    queries, mixer_queries, gate_values = hbm(queries), hbm(mixer_queries), hbm(gate_values)

    k_own, vt_own, kv, msg, cum, mv, mk = call(
        prep_kernel,
        info,
        (keys, values, mixer_values, mixer_keys, step_size, decay_rate),
        [HBM, HBM, HBM, HBM, full((HEADS, TOK)), SMEM],
        [full((TOK, HD))] * 3 + [full((MSG, HD)), full((16, TOK))] + [full((TOK, HD))] * 2,
        [shape((TOK, HD), BF)] * 3 + [shape((MSG, HD), BF), shape((16, TOK), F32)] + [shape((TOK, HD), BF)] * 2,
        scratch=[pltpu.VMEM((TOK, HD), BF), pltpu.SemaphoreType.DMA((4,))],
        flops=US,
    )
    msgs = [msg] + [along_y(msg, d) for d in (1, 2, 3)]
    kv_far = lo(kv)

    y_in = call(
        intra_kernel,
        info,
        (cum, mixer_queries, mk, mv, skip_gain),
        [full((16, TOK)), full((TOK, ROWS)), full((TOK, HD)), full((TOK, HD)), SMEM],
        full((TOK, ROWS)),
        shape((TOK, ROWS), F32),
        flops=US,
    )
    best, acc = call(
        diagonal_kernel,
        info,
        (queries, k_own, vt_own),
        [full((TOK, ROWS)), full((TOK, HD)), full((TOK, HD))],
        [full((8, 8, HALF)), full((8, ACC, HALF))],
        [shape((8, 8, HALF), F32), shape((8, ACC, HALF), F32)],
        flops=US,
    )
    block = lambda zz, xx, half: ((zz % 4) * 4 + (xx % 2) * 2 + c) * 2 + half
    columns = jnp.stack(
        [block(i, x + 1, 1) for i in range(4)]
        + [block(z + d, i, 0) for d in (1, 2, 3) for i in range(2)]
        + [block(z, x + 1, 0)]
        + [block(z + d, x, 1) for d in (1, 2, 3)]
        + [block(z, x, 0), block(z, x, 1)]
    ).astype(jnp.int32)
    weights = call(
        weights_kernel,
        info,
        (hbm(out_weight), hbm(far_weight)),
        [HBM, HBM],
        VMEM,
        pltpu.VMEM((16, 2 * TOK, CB), BF),
        scratch=[pltpu.SemaphoreType.DMA((2, 16))],
        flops=US,
        extra=(columns,),
        after=(acc, y_in),
    )
    prefix, pdec, total, kv_pair = call(
        combine_kernel,
        info,
        (*msgs, kv, kv_far),
        [full((MSG, HD))] * 4 + [full((TOK, HD))] * 2,
        [full((ROWS, HD)), full((8, HD)), full((MSG, HD)), full((2 * TOK, HD))],
        [shape((ROWS, HD), F32), shape((8, HD), F32), shape((MSG, HD), BF), shape((2 * TOK, HD), BF)],
        flops=US,
        after=(y_in, acc, weights),
    )
    total_far = lo(total)
    from_y = [along_y(kv_pair, d) for d in (1, 2, 3)]
    *gated, final_states = call(
        gate_kernel,
        info,
        (cum, mixer_queries, y_in, gate_values, prefix, pdec, total, total_far),
        [
            full((16, TOK)),
            full((TOK, ROWS)),
            full((TOK, ROWS)),
            full((TOK, ROWS)),
            full((ROWS, HD)),
            full((8, HD)),
            full((MSG, HD)),
            full((MSG, HD)),
        ],
        [full((TOK, HD))] * 4 + [full((HEADS, HD // 8, NST))],
        [shape((TOK, HD), BF)] * 4 + [shape((HEADS, HD // 8, NST), F32)],
        flops=US,
    )
    gated += [core(a) for a in gated]

    to_x, *to_z = call(
        first_kernel,
        info,
        (*gated, weights),
        [VMEM] * 9,
        [VMEM] * 4,
        [shape((4, TOK, CB), BF)] + [shape((2, TOK, CB), BF)] * 3,
        flops=US,
        after=from_y,
    )
    from_x = lax.ppermute(to_x, "head", X_SWAP)
    from_z = [along_z(to_z[d - 1], d) for d in (1, 2, 3)]

    mine = [kv, kv_far] + from_y
    other = [core(a) for a in mine]
    pieces = [full((TOK, HD))] * 2 + [full((2 * TOK, HD))] * 3
    k_all, v_all = call(
        place_kernel,
        info,
        (*mine, *other),
        pieces * 2,
        [full((8 * TOK, HD))] * 2,
        [shape((8 * TOK, HD), BF)] * 2,
        flops=US,
        after=(to_z[0],),
    )

    def earlier(heads, first, after, prior=None):
        part = lambda *dims: pl.BlockSpec((2 * heads, *dims), lambda i, info: (first // heads, 0, 0))
        column = pl.BlockSpec((TOK, heads * HD), lambda i, info: (0, first // heads))
        return call(
            lambda *refs: earlier_kernel(heads, *refs),
            info,
            (queries, k_all, v_all, best, acc),
            [column, full((8 * TOK, HD)), full((8 * TOK, HD)), part(8, HALF), part(ACC, HALF)],
            column,
            shape((TOK, ROWS), BF),
            flops=US,
            after=after if prior is None else (prior, *after),
            alias=None if prior is None else 0,
        )

    attended = earlier(2, 0, (to_z[0],))

    to_x2, *to_z2 = call(
        second_kernel,
        info,
        (*gated, weights, *from_z, from_x),
        [VMEM] * 13,
        [VMEM] * 4,
        [shape((TOK, CB), BF)] * 4,
        flops=US,
        after=(attended,),
    )
    from_x2 = lax.ppermute(to_x2, "head", X_SWAP)
    from_z2 = [along_z(to_z2[d - 1], d) for d in (1, 2, 3)]
    kept = call(
        keep_kernel,
        info,
        (*gated, weights, *from_z, from_x),
        [VMEM] * 13,
        VMEM,
        shape((TOK, ROWS), F32),
        flops=US,
        after=(to_x2,),
    )
    attended = earlier(2, 2, (to_x2,), attended)
    summed = call(
        finish_kernel,
        info,
        (kept, from_x2, *from_z2),
        [full((TOK, ROWS))] + [full((TOK, CB))] * 4,
        full((TOK, ROWS)),
        shape((TOK, ROWS), BF),
        flops=US,
        after=(attended,),
    )
    return (attended, summed, final_states)


def solution(mesh):
    placed = (
        P("seq", "head"),
        P("seq", None),
        P("seq", None),
        P(),
        P("seq", None),
        P("seq", None),
        P("seq", "head"),
        P("seq", "head"),
        P("head", "seq"),
        P("head"),
        P("head"),
        P("head", None),
    )
    return jax.shard_map(
        body,
        mesh=mesh,
        in_specs=placed,
        out_specs=(P("seq", "head"), P("seq", "head"), P("head", "seq", None)),
        check_vma=False,
    )
```

```python
import math

import jax
import jax.numpy as jnp
from jax import lax
from jax.experimental import pallas as pl
from jax.experimental.pallas import tpu as pltpu
from jax.sharding import PartitionSpec as P

H = 64
KVH = 8
HD = 128
NST = 128
TOK = 512
HEADS = 4
ROWS = HEADS * HD
MSG = ROWS + 32
CB = 256
BF = jnp.bfloat16
F32 = jnp.float32
US = 10**5
NT = (((1,), (1,)), ((), ()))
VMEM_LIMIT = 16 * 1024 * 1024

SEQ, CORE, GROUP, LENGTH, YPOS, XLO, ZPOS, XHI, COLUMNS = range(9)


def call(kernel, info, args, in_specs, out_specs, out_shape, grid=(1,), scratch=(), flops=0, nbytes=0, trans=0, extra=(), after=(), limit=VMEM_LIMIT, alias=None):
    scalars = 1 + len(extra)
    first = scalars + len(args)

    def run(*refs):
        kernel(*refs[:first], *refs[first + len(after) :])

    aliases = {} if alias is None else {first + alias: 0}

    spec = pltpu.PrefetchScalarGridSpec(
        num_scalar_prefetch=scalars,
        grid=grid,
        in_specs=[*in_specs, *[ANY] * len(after)],
        out_specs=out_specs,
        scratch_shapes=list(scratch),
    )
    return pl.pallas_call(
        run,
        grid_spec=spec,
        out_shape=out_shape,
        input_output_aliases=aliases,
        compiler_params=pltpu.CompilerParams(vmem_limit_bytes=limit),
        cost_estimate=pl.CostEstimate(flops=flops, bytes_accessed=nbytes, transcendentals=trans),
    )(info, *extra, *args, *after)


def full(shape):
    return pl.BlockSpec(shape, lambda i, *_: (0,) * len(shape))


def hbm(a):
    return pltpu.with_memory_space_constraint(a, pltpu.HBM)


ANY = pl.BlockSpec(memory_space=pl.ANY)
HBM = pl.BlockSpec(memory_space=pltpu.HBM)
VMEM = pl.BlockSpec(memory_space=pltpu.VMEM)
SMEM = pl.BlockSpec(memory_space=pltpu.SMEM)


def shape(dims, kind):
    return jax.ShapeDtypeStruct(dims, kind)


def kept_shape(dims, kind):
    return pltpu.VMEM(dims, kind)


def split2(a):
    high = a.astype(BF)
    return high, (a - high.astype(F32)).astype(BF)


def prep_kernel(
    info, k_hbm, v_hbm, mv_hbm, mk_hbm, step_ref, rate_ref, k_ref, vt_ref, kv_ref, msg_ref, cum_ref, mv_ref, mk_ref, v_ref, sems
):
    columns = pl.ds(pl.multiple_of(info[GROUP] * HD, HD), HD)
    pairs = ((mv_hbm, mv_ref), (mk_hbm, mk_ref), (k_hbm, k_ref), (v_hbm, v_ref))
    copies = [pltpu.make_async_copy(a.at[:, columns], b, sems.at[i]) for i, (a, b) in enumerate(pairs)]
    for copy in copies:
        copy.start()

    row = lax.broadcasted_iota(jnp.int32, (8, TOK), 0)
    lane = lax.broadcasted_iota(jnp.int32, (8, TOK), 1)
    step = jnp.concatenate([step_ref[...], jnp.zeros((8 - HEADS, TOK), F32)], axis=0)
    step = jnp.where(info[SEQ] * TOK + lane < info[LENGTH], step, 0.0)
    rate = jnp.zeros((8, TOK), F32)
    for h in range(HEADS):
        rate = jnp.where(row == h, rate_ref[h], rate)
    cum = -step * rate
    shift = 1
    while shift < TOK:
        cum = cum + jnp.where(lane >= shift, pltpu.roll(cum, shift, 1), 0.0)
        shift *= 2
    cum_ref[0:8, :] = cum
    cum_ref[8:16, :] = step
    last = cum[:, TOK - 1 : TOK]
    tail = jnp.exp(last - cum) * step
    log = jnp.broadcast_to(last, (8, HD))
    high = log.astype(BF).astype(F32)
    mid = (log - high).astype(BF).astype(F32)
    low = log - high - mid
    msg_ref[ROWS:MSG, :] = jnp.concatenate([high, mid, low, jnp.zeros_like(low)], axis=0).astype(BF)
    copies[0].wait()
    copies[1].wait()
    vt = mv_ref[...].astype(F32).T
    mk = mk_ref[...]
    for h in range(HEADS):
        high, low = split2(vt * tail[h : h + 1, :])
        state = jnp.dot(high, mk, preferred_element_type=F32) + jnp.dot(low, mk, preferred_element_type=F32)
        msg_ref[h * HD : (h + 1) * HD, :] = state.astype(BF)
    copies[2].wait()
    copies[3].wait()
    zero = info[CORE] == 0
    for i in range(TOK // HD):
        part = pl.ds(i * HD, HD)
        turned = v_ref[part, :].astype(F32).T
        vt_ref[part, :] = turned.astype(BF)
        kv_ref[part, :] = jnp.where(zero, k_ref[part, :].astype(F32), turned).astype(BF)


def log_of(msg):
    tail = msg[ROWS:MSG, :].astype(F32)
    return tail[0:8] + tail[8:16] + tail[16:24]


def combine_kernel(info, m0, m1, m2, m3, kv, kv_far, prefix_ref, pdec_ref, total_ref, pair_ref):
    pair_ref[0:TOK, :] = kv[...]
    pair_ref[TOK : 2 * TOK, :] = kv_far[...]
    y = info[YPOS]
    msgs = (m0, m1, m2, m3)
    place = [lax.rem(y - d + 4, 4) for d in range(4)]
    logs = [log_of(m) for m in msgs]
    pre, tot = [], []
    for d in range(4):
        in_pre = jnp.zeros_like(logs[0])
        in_tot = jnp.zeros_like(logs[0])
        for e in range(4):
            if e == d:
                continue
            after = place[e] > place[d]
            in_tot = in_tot + jnp.where(after, logs[e], 0.0)
            in_pre = in_pre + jnp.where(jnp.logical_and(after, place[e] < y), logs[e], 0.0)
        tot.append(jnp.exp(in_tot))
        pre.append(jnp.where(place[d] < y, jnp.exp(in_pre), 0.0))
    whole = logs[0] + logs[1] + logs[2] + logs[3]
    before = jnp.zeros_like(whole)
    for e in range(4):
        before = before + jnp.where(place[e] < y, logs[e], 0.0)
    pdec_ref[...] = jnp.exp(before)
    for h in range(HEADS):
        part = slice(h * HD, (h + 1) * HD)
        own = [m[part, :].astype(F32) for m in msgs]
        total = own[0] * tot[0][h : h + 1]
        prefix = own[1] * pre[1][h : h + 1]
        for d in range(1, 4):
            total = total + own[d] * tot[d][h : h + 1]
        for d in range(2, 4):
            prefix = prefix + own[d] * pre[d][h : h + 1]
        prefix_ref[part, :] = prefix
        total_ref[part, :] = total.astype(BF)
    high = whole.astype(BF).astype(F32)
    mid = (whole - high).astype(BF).astype(F32)
    low = whole - high - mid
    total_ref[ROWS:MSG, :] = jnp.concatenate([high, mid, low, jnp.zeros_like(low)], axis=0).astype(BF)


def intra_kernel(info, cum_ref, c_ref, mk_ref, mv_ref, skip_ref, y_ref):
    cum = cum_ref[0:8, :]
    step = cum_ref[8:16, :]
    cols = cum.T
    half = TOK // 2
    for h in range(HEADS):
        part = slice(h * HD, (h + 1) * HD)
        for i in range(2):
            here = slice(i * half, (i + 1) * half)
            wide = (i + 1) * half
            inner = lax.dot_general(c_ref[here, part], mk_ref[0:wide, :], NT, preferred_element_type=F32)
            t = i * half + lax.broadcasted_iota(jnp.int32, (half, wide), 0)
            s = lax.broadcasted_iota(jnp.int32, (half, wide), 1)
            diff = jnp.where(s <= t, cols[here, h : h + 1] - cum[h : h + 1, 0:wide], -jnp.inf)
            mix = (jnp.exp(diff) * inner * step[h : h + 1, 0:wide]).astype(BF)
            y = jnp.dot(mix, mv_ref[0:wide, :], preferred_element_type=F32)
            y_ref[here, part] = y + skip_ref[h] * mv_ref[here, :].astype(F32)


def gate_kernel(info, cum_ref, c_ref, y_ref, g_ref, prefix_ref, pdec_ref, own_ref, got_ref, out0, out1, fin_ref):
    second = info[XLO] == 1
    ecols = jnp.exp(cum_ref[0:8, :]).T
    for h in range(HEADS):
        part = slice(h * HD, (h + 1) * HD)
        far = pdec_ref[h : h + 1, :] * got_ref[part, :].astype(F32)
        state = prefix_ref[part, :] + jnp.where(second, far, 0.0)
        high, low = split2(state)
        c = c_ref[:, part]
        carried = lax.dot_general(
            jnp.concatenate([c, c], axis=1), jnp.concatenate([high, low], axis=1), NT, preferred_element_type=F32
        )
        y = y_ref[:, part] + ecols[:, h : h + 1] * carried
        g = g_ref[:, part].astype(F32)
        (out0, out1)[h // 2][:, (h % 2) * HD : (h % 2 + 1) * HD] = (y * (g / (1.0 + jnp.exp(-g)))).astype(BF)
    own_log = log_of(own_ref)
    got_log = log_of(got_ref)
    later = jnp.exp(jnp.where(second, own_log, got_log))
    for h in range(HEADS):
        rows = pl.ds(pl.multiple_of(h * HD + info[SEQ] * (HD // 8), HD // 8), HD // 8)
        own = own_ref[rows, :].astype(F32)
        got = got_ref[rows, :].astype(F32)
        first = jnp.where(second, got, own)
        last = jnp.where(second, own, got)
        fin_ref[h] = last + later[h : h + 1, :] * first


SCALE = math.log2(math.e) / math.sqrt(HD)
HALF = TOK // 2
UNITS = [(h, i) for h in range(HEADS) for i in range(2)]
ACC = HD + 16


def with_ones(panels):
    vt = jnp.concatenate(panels, axis=1)
    return jnp.concatenate([vt, jnp.ones((16, vt.shape[1]), BF)], axis=0)


def split_pair(info, mine, other):
    zero = jnp.broadcast_to(info[CORE], mine.shape) == 0
    a, b = mine.astype(F32), other.astype(F32)
    return jnp.where(zero, a, b).astype(BF), jnp.where(zero, b, a).astype(BF)


def pieces(q_ref):
    return [q_ref[i * HALF : (i + 1) * HALF, h * HD : (h + 1) * HD] for h, i in UNITS]


def add_block(queries, k, v, state):
    vt = with_ones([v[i * HD : (i + 1) * HD] for i in range(TOK // HD)])
    scores = [lax.dot_general(k, q, NT, preferred_element_type=F32) for q in queries]
    new = []
    for u in range(len(UNITS)):
        best, summed = state[2 * u], state[2 * u + 1]
        top = jnp.maximum(best, jnp.max(scores[u], axis=0, keepdims=True))
        weights = jnp.exp2((scores[u] - top) * SCALE).astype(BF)
        shrink = jnp.exp2((best - top) * SCALE)
        new += [top, summed * shrink + jnp.dot(vt, weights, preferred_element_type=F32)]
    return tuple(new)


def diagonal_kernel(info, q_ref, k_ref, v_ref, best_ref, acc_ref):
    limit = info[LENGTH] - info[SEQ] * TOK
    vt = with_ones([v_ref[i * HD : (i + 1) * HD, :] for i in range(TOK // HD)])
    queries = pieces(q_ref)
    for u, (h, i) in enumerate(UNITS):
        wide = (i + 1) * HALF
        scores = lax.dot_general(k_ref[0:wide, :], queries[u], NT, preferred_element_type=F32)
        s = lax.broadcasted_iota(jnp.int32, (wide, HALF), 0)
        t = i * HALF + lax.broadcasted_iota(jnp.int32, (wide, HALF), 1)
        keep = jnp.logical_and(s <= t, s < limit)
        scores = jnp.where(keep, scores, -jnp.inf)
        best = jnp.max(scores, axis=0, keepdims=True)
        weights = jnp.exp2((scores - best) * SCALE).astype(BF)
        best_ref[u] = jnp.broadcast_to(best, (8, HALF))
        acc_ref[u] = jnp.dot(vt[:, 0:wide], weights, preferred_element_type=F32)


def earlier_kernel(info, q_ref, far, far_other, mine, other, best_ref, acc_ref, out_ref, k_all, v_all):
    y, x = info[YPOS], info[XLO]
    place = (1 - x) * 4 + y
    k_all[place], v_all[place] = split_pair(info, far[...], far_other[...])
    for d in (1, 2, 3):
        for plane, rows in ((x, slice(0, TOK)), (1 - x, slice(TOK, 2 * TOK))):
            place = plane * 4 + lax.rem(y - d + 4, 4)
            k_all[place], v_all[place] = split_pair(info, mine[d - 1, rows, :], other[d - 1, rows, :])
    queries = pieces(q_ref)
    start = []
    for u in range(len(UNITS)):
        start += [best_ref[u, 0:1, :], acc_ref[u]]
    state = lax.fori_loop(
        0, info[SEQ], lambda j, state: add_block(queries, k_all[j], v_all[j], state), tuple(start)
    )
    for u, (h, i) in enumerate(UNITS):
        summed = state[2 * u + 1]
        out = summed[0:HD] * (1.0 / summed[HD : HD + 1])
        out_ref[i * HALF : (i + 1) * HALF, h * HD : (h + 1) * HD] = out.T.astype(BF)


def weights_kernel(info, near, far, out_ref, sems):
    def copies(k):
        part = pl.ds(pl.multiple_of(info[COLUMNS + k] * CB, CB), CB)
        return (
            pltpu.make_async_copy(near.at[:, part], out_ref.at[k, 0:TOK, :], sems.at[0, k]),
            pltpu.make_async_copy(far.at[:, part], out_ref.at[k, TOK : 2 * TOK, :], sems.at[1, k]),
        )

    for k in range(16):
        for copy in copies(k):
            copy.start()
    for k in range(16):
        for copy in copies(k):
            copy.wait()


def product(gated, weights, first, n):
    g = jnp.concatenate([r[...] for r in gated], axis=1)
    w = jnp.concatenate([weights[first + k] for k in range(n)], axis=1)
    return jnp.dot(g, w, preferred_element_type=F32)


def first_kernel(info, *refs):
    gated, weights, got, to_x, to_z, bundle = refs[0:4], refs[4], refs[5:8], refs[8], refs[9:12], refs[12]
    for d in range(3):
        bundle[d] = got[d][...]
    for i in range(2):
        acc = product(gated, weights, 2 * i, 2).astype(BF)
        to_x[2 * i] = acc[:, 0:CB]
        to_x[2 * i + 1] = acc[:, CB : 2 * CB]
    for d in range(3):
        acc = product(gated, weights, 4 + 2 * d, 2).astype(BF)
        to_z[d][0] = acc[:, 0:CB]
        to_z[d][1] = acc[:, CB : 2 * CB]


def second_kernel(info, *refs):
    gated, (weights, z1, z2, z3, x, to_x), to_z = refs[0:4], refs[4:10], refs[10:13]
    acc = product(gated, weights, 10, 2)
    total = acc[:, 0:CB]
    for r in (z1, z2, z3):
        total = total + r[1 - info[XHI]].astype(F32)
    to_x[...] = total.astype(BF)
    part = acc[:, CB : 2 * CB]
    to_z[0][...] = (part + x[lax.rem(info[ZPOS] + 1, 4)].astype(F32)).astype(BF)
    acc = product(gated, weights, 12, 2)
    for d in (1, 2):
        part = acc[:, (d - 1) * CB : d * CB]
        to_z[d][...] = (part + x[lax.rem(info[ZPOS] + d + 1, 4)].astype(F32)).astype(BF)


def keep_kernel(info, *refs):
    gated, (weights, z1, z2, z3, x, out_ref) = refs[0:4], refs[4:10]
    acc = product(gated, weights, 14, 2)
    total = acc[:, 0:CB]
    for r in (z1, z2, z3):
        total = total + r[info[XHI]].astype(F32)
    out_ref[:, 0:CB] = total
    out_ref[:, CB : 2 * CB] = acc[:, CB : 2 * CB] + x[info[ZPOS]].astype(F32)


def finish_kernel(info, kept, x, z1, z2, z3, out_ref):
    out_ref[:, 0:CB] = (kept[:, 0:CB] + x[...].astype(F32)).astype(BF)
    total = kept[:, CB : 2 * CB]
    for r in (z1, z2, z3):
        total = total + r[...].astype(F32)
    out_ref[:, CB : 2 * CB] = total.astype(BF)


def head_perm(move):
    pairs = []
    for z in range(4):
        for x in range(2):
            for c in range(2):
                z2, x2, c2 = move(z, x, c)
                pairs.append((z * 4 + x * 2 + c, (z2 % 4) * 4 + (x2 % 2) * 2 + c2 % 2))
    return pairs


CORE_SWAP = head_perm(lambda z, x, c: (z, x, c + 1))
X_SWAP = head_perm(lambda z, x, c: (z, x + 1, c))
Z_MOVE = {d: head_perm(lambda z, x, c, d=d: (z + d, x, c)) for d in (1, 2, 3)}
LO_SWAP = [(i, (i + 4) % 8) for i in range(8)]
Y_MOVE = {d: [(x * 4 + y, x * 4 + (y + d) % 4) for x in range(2) for y in range(4)] for d in (1, 2, 3)}


def body(
    queries,
    keys,
    values,
    length,
    mixer_values,
    mixer_keys,
    mixer_queries,
    gate_values,
    step_size,
    decay_rate,
    skip_gain,
    out_weight,
):
    seq = lax.axis_index("seq")
    head = lax.axis_index("head")
    z, x, c = head // 4, (head // 2) % 2, head % 2
    block = lambda zz, xx, half: ((zz % 4) * 4 + (xx % 2) * 2 + c) * 2 + half
    columns = (
        [block(i, x + 1, 1) for i in range(4)]
        + [block(z + d, i, 0) for d in (1, 2, 3) for i in range(2)]
        + [block(z, x + 1, 0)]
        + [block(z + d, x, 1) for d in (1, 2, 3)]
        + [block(z, x, 0), block(z, x, 1)]
    )
    info = jnp.stack([seq, c, head // 2, length[0], seq % 4, seq // 4, z, x, *columns]).astype(jnp.int32)
    core = lambda a: lax.ppermute(a, "head", CORE_SWAP)
    lo = lambda a: lax.ppermute(a, "seq", LO_SWAP)
    along_y = lambda a, d: lax.ppermute(a, "seq", Y_MOVE[d])
    along_z = lambda a, d: lax.ppermute(a, "head", Z_MOVE[d])

    far_weight = core(out_weight)
    keys, values, mixer_values, mixer_keys = hbm(keys), hbm(values), hbm(mixer_values), hbm(mixer_keys)
    step_size, decay_rate, skip_gain = hbm(step_size), hbm(decay_rate), hbm(skip_gain)

    k_own, vt_own, kv, msg, cum, mv, mk = call(
        prep_kernel,
        info,
        (keys, values, mixer_values, mixer_keys, step_size, decay_rate),
        [HBM, HBM, HBM, HBM, full((HEADS, TOK)), SMEM],
        [full((TOK, HD))] * 3 + [full((MSG, HD)), full((16, TOK))] + [full((TOK, HD))] * 2,
        [kept_shape((TOK, HD), BF)] * 3 + [kept_shape((MSG, HD), BF), kept_shape((16, TOK), F32)] + [kept_shape((TOK, HD), BF)] * 2,
        scratch=[pltpu.VMEM((TOK, HD), BF), pltpu.SemaphoreType.DMA((4,))],
        flops=US,
    )
    from_1, from_3, from_2 = [along_y(msg, d) for d in (1, 3, 2)]
    msgs = [msg, from_1, from_2, from_3]
    kv_far = lo(kv)
    kv_far_other = core(kv_far)

    y_in = call(
        intra_kernel,
        info,
        (cum, hbm(mixer_queries), mk, mv, skip_gain),
        [full((16, TOK)), full((TOK, ROWS)), full((TOK, HD)), full((TOK, HD)), SMEM],
        full((TOK, ROWS)),
        kept_shape((TOK, ROWS), F32),
        flops=US,
    )
    best, acc = call(
        diagonal_kernel,
        info,
        (hbm(queries), k_own, vt_own),
        [full((TOK, ROWS)), full((TOK, HD)), full((TOK, HD))],
        [full((8, 8, HALF)), full((8, ACC, HALF))],
        [kept_shape((8, 8, HALF), F32), kept_shape((8, ACC, HALF), F32)],
        flops=US,
    )
    prefix, pdec, total, kv_pair = call(
        combine_kernel,
        info,
        (*msgs, kv, kv_far),
        [full((MSG, HD))] * 4 + [full((TOK, HD))] * 2,
        [full((ROWS, HD)), full((8, HD)), full((MSG, HD)), full((2 * TOK, HD))],
        [kept_shape((ROWS, HD), F32), kept_shape((8, HD), F32), kept_shape((MSG, HD), BF), kept_shape((2 * TOK, HD), BF)],
        flops=US,
        after=(y_in, acc),
    )
    total_far = lo(total)
    from_1, from_3, from_2 = [along_y(kv_pair, d) for d in (1, 3, 2)]
    from_y = [from_1, from_2, from_3]
    *gated, final_states = call(
        gate_kernel,
        info,
        (cum, mixer_queries, y_in, gate_values, prefix, pdec, total, total_far),
        [
            full((16, TOK)),
            full((TOK, ROWS)),
            full((TOK, ROWS)),
            full((TOK, ROWS)),
            full((ROWS, HD)),
            full((8, HD)),
            full((MSG, HD)),
            full((MSG, HD)),
        ],
        [full((TOK, 2 * HD))] * 2 + [full((HEADS, HD // 8, NST))],
        [shape((TOK, 2 * HD), BF)] * 2 + [shape((HEADS, HD // 8, NST), F32)],
        flops=US,
    )
    weights = call(
        weights_kernel,
        info,
        (hbm(out_weight), hbm(far_weight)),
        [HBM, HBM],
        VMEM,
        pltpu.VMEM((16, 2 * TOK, CB), BF),
        scratch=[pltpu.SemaphoreType.DMA((2, 16))],
        flops=10**10,
        after=(gated[0],),
    )
    gated += [core(a) for a in gated]

    to_x, *to_z, bundle = call(
        first_kernel,
        info,
        (*gated, weights, *from_y),
        [VMEM] * 8,
        [VMEM] * 5,
        [shape((4, TOK, CB), BF)] + [shape((2, TOK, CB), BF)] * 3 + [shape((3, 2 * TOK, HD), BF)],
        flops=US,
    )
    from_x = lax.ppermute(to_x, "head", X_SWAP)
    from_1, from_3, from_2 = [along_z(to_z[d - 1], d) for d in (1, 3, 2)]
    from_z = [from_1, from_2, from_3]

    attended = call(
        earlier_kernel,
        info,
        (queries, kv_far, kv_far_other, bundle, core(bundle), best, acc),
        [full((TOK, ROWS))] + [full((TOK, HD))] * 2 + [full((3, 2 * TOK, HD))] * 2 + [full((8, 8, HALF)), full((8, ACC, HALF))],
        full((TOK, ROWS)),
        shape((TOK, ROWS), BF),
        scratch=[pltpu.VMEM((8, TOK, HD), BF)] * 2,
        flops=US,
        limit=28 * 1024 * 1024,
        after=(to_z[0],),
    )

    to_x2, *to_z2 = call(
        second_kernel,
        info,
        (*gated, weights, *from_z, from_x),
        [VMEM] * 9,
        [VMEM] * 4,
        [shape((TOK, CB), BF)] * 4,
        flops=US,
        after=(hbm(attended),),
    )
    from_1, from_3, from_2 = [along_z(to_z2[d - 1], d) for d in (1, 3, 2)]
    from_z2 = [from_1, from_2, from_3]
    from_x2 = lax.ppermute(to_x2, "head", X_SWAP)
    kept = call(
        keep_kernel,
        info,
        (*gated, weights, *from_z, from_x),
        [VMEM] * 9,
        VMEM,
        shape((TOK, ROWS), F32),
        flops=US,
        after=(to_x2,),
    )
    summed = call(
        finish_kernel,
        info,
        (kept, from_x2, *from_z2),
        [full((TOK, ROWS))] + [full((TOK, CB))] * 4,
        full((TOK, ROWS)),
        shape((TOK, ROWS), BF),
        flops=US,
    )
    return (attended, summed, final_states)


def solution(mesh):
    placed = (
        P("seq", "head"),
        P("seq", None),
        P("seq", None),
        P(),
        P("seq", None),
        P("seq", None),
        P("seq", "head"),
        P("seq", "head"),
        P("head", "seq"),
        P("head"),
        P("head"),
        P("head", None),
    )
    return jax.shard_map(
        body,
        mesh=mesh,
        in_specs=placed,
        out_specs=(P("seq", "head"), P("seq", "head"), P("head", "seq", None)),
        check_vma=False,
    )
```

```python
import math

import jax
import jax.numpy as jnp
from jax import lax
from jax.experimental import pallas as pl
from jax.experimental.pallas import tpu as pltpu
from jax.sharding import PartitionSpec as P

H = 64
KVH = 8
HD = 128
NST = 128
TOK = 512
HEADS = 4
ROWS = HEADS * HD
MSG = ROWS + 32
CB = 256
Z_ORDER = (2, 1, 3)
BF = jnp.bfloat16
F32 = jnp.float32
US = 10**5
NT = (((1,), (1,)), ((), ()))
VMEM_LIMIT = 16 * 1024 * 1024

SEQ, CORE, GROUP, LENGTH, YPOS, XLO, ZPOS, XHI, COLUMNS = range(9)


def call(kernel, info, args, in_specs, out_specs, out_shape, grid=(1,), scratch=(), flops=0, nbytes=0, trans=0, extra=(), after=(), limit=VMEM_LIMIT, alias=None):
    scalars = 1 + len(extra)
    first = scalars + len(args)

    def run(*refs):
        kernel(*refs[:first], *refs[first + len(after) :])

    aliases = {} if alias is None else {first + alias: 0}

    spec = pltpu.PrefetchScalarGridSpec(
        num_scalar_prefetch=scalars,
        grid=grid,
        in_specs=[*in_specs, *[ANY] * len(after)],
        out_specs=out_specs,
        scratch_shapes=list(scratch),
    )
    return pl.pallas_call(
        run,
        grid_spec=spec,
        out_shape=out_shape,
        input_output_aliases=aliases,
        compiler_params=pltpu.CompilerParams(vmem_limit_bytes=limit),
        cost_estimate=pl.CostEstimate(flops=flops, bytes_accessed=nbytes, transcendentals=trans),
    )(info, *extra, *args, *after)


def full(shape):
    return pl.BlockSpec(shape, lambda i, *_: (0,) * len(shape))


def hbm(a):
    return pltpu.with_memory_space_constraint(a, pltpu.HBM)


ANY = pl.BlockSpec(memory_space=pl.ANY)
HBM = pl.BlockSpec(memory_space=pltpu.HBM)
VMEM = pl.BlockSpec(memory_space=pltpu.VMEM)
SMEM = pl.BlockSpec(memory_space=pltpu.SMEM)


def shape(dims, kind):
    return jax.ShapeDtypeStruct(dims, kind)


def kept_shape(dims, kind):
    return pltpu.VMEM(dims, kind)


def split2(a):
    high = a.astype(BF)
    return high, (a - high.astype(F32)).astype(BF)


def prep_kernel(
    info, k_hbm, v_hbm, mv_hbm, mk_hbm, step_ref, rate_ref, k_ref, vt_ref, kv_ref, msg_ref, cum_ref, mv_ref, mk_ref, v_ref, sems
):
    columns = pl.ds(pl.multiple_of(info[GROUP] * HD, HD), HD)
    pairs = ((mv_hbm, mv_ref), (mk_hbm, mk_ref), (k_hbm, k_ref), (v_hbm, v_ref))
    copies = [pltpu.make_async_copy(a.at[:, columns], b, sems.at[i]) for i, (a, b) in enumerate(pairs)]
    for copy in copies:
        copy.start()

    row = lax.broadcasted_iota(jnp.int32, (8, TOK), 0)
    lane = lax.broadcasted_iota(jnp.int32, (8, TOK), 1)
    step = jnp.concatenate([step_ref[...], jnp.zeros((8 - HEADS, TOK), F32)], axis=0)
    step = jnp.where(info[SEQ] * TOK + lane < info[LENGTH], step, 0.0)
    rate = jnp.zeros((8, TOK), F32)
    for h in range(HEADS):
        rate = jnp.where(row == h, rate_ref[h], rate)
    cum = -step * rate
    shift = 1
    while shift < TOK:
        cum = cum + jnp.where(lane >= shift, pltpu.roll(cum, shift, 1), 0.0)
        shift *= 2
    cum_ref[0:8, :] = cum
    cum_ref[8:16, :] = step
    last = cum[:, TOK - 1 : TOK]
    tail = jnp.exp(last - cum) * step
    log = jnp.broadcast_to(last, (8, HD))
    high = log.astype(BF).astype(F32)
    mid = (log - high).astype(BF).astype(F32)
    low = log - high - mid
    msg_ref[ROWS:MSG, :] = jnp.concatenate([high, mid, low, jnp.zeros_like(low)], axis=0).astype(BF)
    copies[0].wait()
    copies[1].wait()
    vt = mv_ref[...].astype(F32).T
    mk = mk_ref[...]
    for h in range(HEADS):
        high, low = split2(vt * tail[h : h + 1, :])
        state = jnp.dot(high, mk, preferred_element_type=F32) + jnp.dot(low, mk, preferred_element_type=F32)
        msg_ref[h * HD : (h + 1) * HD, :] = state.astype(BF)
    copies[2].wait()
    copies[3].wait()
    zero = info[CORE] == 0
    for i in range(TOK // HD):
        part = pl.ds(i * HD, HD)
        turned = v_ref[part, :].astype(F32).T
        vt_ref[part, :] = turned.astype(BF)
        kv_ref[part, :] = jnp.where(zero, k_ref[part, :].astype(F32), turned).astype(BF)


def log_of(msg):
    tail = msg[ROWS:MSG, :].astype(F32)
    return tail[0:8] + tail[8:16] + tail[16:24]


def combine_kernel(info, m0, m1, m2, m3, kv, kv_far, prefix_ref, pdec_ref, total_ref, pair_ref):
    pair_ref[0:TOK, :] = kv[...]
    pair_ref[TOK : 2 * TOK, :] = kv_far[...]
    y = info[YPOS]
    msgs = (m0, m1, m2, m3)
    place = [lax.rem(y - d + 4, 4) for d in range(4)]
    logs = [log_of(m) for m in msgs]
    pre, tot = [], []
    for d in range(4):
        in_pre = jnp.zeros_like(logs[0])
        in_tot = jnp.zeros_like(logs[0])
        for e in range(4):
            if e == d:
                continue
            after = place[e] > place[d]
            in_tot = in_tot + jnp.where(after, logs[e], 0.0)
            in_pre = in_pre + jnp.where(jnp.logical_and(after, place[e] < y), logs[e], 0.0)
        tot.append(jnp.exp(in_tot))
        pre.append(jnp.where(place[d] < y, jnp.exp(in_pre), 0.0))
    whole = logs[0] + logs[1] + logs[2] + logs[3]
    before = jnp.zeros_like(whole)
    for e in range(4):
        before = before + jnp.where(place[e] < y, logs[e], 0.0)
    pdec_ref[...] = jnp.exp(before)
    for h in range(HEADS):
        part = slice(h * HD, (h + 1) * HD)
        own = [m[part, :].astype(F32) for m in msgs]
        total = own[0] * tot[0][h : h + 1]
        prefix = own[1] * pre[1][h : h + 1]
        for d in range(1, 4):
            total = total + own[d] * tot[d][h : h + 1]
        for d in range(2, 4):
            prefix = prefix + own[d] * pre[d][h : h + 1]
        prefix_ref[part, :] = prefix
        total_ref[part, :] = total.astype(BF)
    high = whole.astype(BF).astype(F32)
    mid = (whole - high).astype(BF).astype(F32)
    low = whole - high - mid
    total_ref[ROWS:MSG, :] = jnp.concatenate([high, mid, low, jnp.zeros_like(low)], axis=0).astype(BF)


def intra_kernel(info, cum_ref, c_ref, mk_ref, mv_ref, skip_ref, y_ref):
    cum = cum_ref[0:8, :]
    step = cum_ref[8:16, :]
    cols = cum.T
    half = TOK // 2
    for h in range(HEADS):
        part = slice(h * HD, (h + 1) * HD)
        for i in range(2):
            here = slice(i * half, (i + 1) * half)
            wide = (i + 1) * half
            inner = lax.dot_general(c_ref[here, part], mk_ref[0:wide, :], NT, preferred_element_type=F32)
            t = i * half + lax.broadcasted_iota(jnp.int32, (half, wide), 0)
            s = lax.broadcasted_iota(jnp.int32, (half, wide), 1)
            diff = jnp.where(s <= t, cols[here, h : h + 1] - cum[h : h + 1, 0:wide], -jnp.inf)
            mix = (jnp.exp(diff) * inner * step[h : h + 1, 0:wide]).astype(BF)
            y = jnp.dot(mix, mv_ref[0:wide, :], preferred_element_type=F32)
            y_ref[here, part] = y + skip_ref[h] * mv_ref[here, :].astype(F32)


def gate_kernel(info, cum_ref, c_ref, y_ref, g_ref, prefix_ref, pdec_ref, own_ref, got_ref, out0, out1, fin_ref):
    second = info[XLO] == 1
    ecols = jnp.exp(cum_ref[0:8, :]).T
    for h in range(HEADS):
        part = slice(h * HD, (h + 1) * HD)
        far = pdec_ref[h : h + 1, :] * got_ref[part, :].astype(F32)
        state = prefix_ref[part, :] + jnp.where(second, far, 0.0)
        high, low = split2(state)
        c = c_ref[:, part]
        carried = lax.dot_general(
            jnp.concatenate([c, c], axis=1), jnp.concatenate([high, low], axis=1), NT, preferred_element_type=F32
        )
        y = y_ref[:, part] + ecols[:, h : h + 1] * carried
        g = g_ref[:, part].astype(F32)
        (out0, out1)[h // 2][:, (h % 2) * HD : (h % 2 + 1) * HD] = (y * (g / (1.0 + jnp.exp(-g)))).astype(BF)
    own_log = log_of(own_ref)
    got_log = log_of(got_ref)
    later = jnp.exp(jnp.where(second, own_log, got_log))
    for h in range(HEADS):
        rows = pl.ds(pl.multiple_of(h * HD + info[SEQ] * (HD // 8), HD // 8), HD // 8)
        own = own_ref[rows, :].astype(F32)
        got = got_ref[rows, :].astype(F32)
        first = jnp.where(second, got, own)
        last = jnp.where(second, own, got)
        fin_ref[h] = last + later[h : h + 1, :] * first


SCALE = math.log2(math.e) / math.sqrt(HD)
HALF = TOK // 2
UNITS = [(h, i) for h in range(HEADS) for i in range(2)]
ACC = HD + 16


def with_ones(panels):
    vt = jnp.concatenate(panels, axis=1)
    return jnp.concatenate([vt, jnp.ones((16, vt.shape[1]), BF)], axis=0)


def split_pair(info, mine, other):
    zero = jnp.broadcast_to(info[CORE], mine.shape) == 0
    a, b = mine.astype(F32), other.astype(F32)
    return jnp.where(zero, a, b).astype(BF), jnp.where(zero, b, a).astype(BF)


def pieces(q_ref):
    return [q_ref[i * HALF : (i + 1) * HALF, h * HD : (h + 1) * HD] for h, i in UNITS]


def add_block(queries, k, v, state):
    vt = with_ones([v[i * HD : (i + 1) * HD] for i in range(TOK // HD)])
    scores = [lax.dot_general(k, q, NT, preferred_element_type=F32) for q in queries]
    new = []
    for u in range(len(UNITS)):
        best, summed = state[2 * u], state[2 * u + 1]
        top = jnp.maximum(best, jnp.max(scores[u], axis=0, keepdims=True))
        weights = jnp.exp2((scores[u] - top) * SCALE).astype(BF)
        shrink = jnp.exp2((best - top) * SCALE)
        new += [top, summed * shrink + jnp.dot(vt, weights, preferred_element_type=F32)]
    return tuple(new)


def earlier_kernel(info, q_ref, far, far_other, mine, other, best_ref, acc_ref, k_all, v_all):
    y, x = info[YPOS], info[XLO]
    place = (1 - x) * 4 + y
    k_all[place], v_all[place] = split_pair(info, far[...], far_other[...])
    for d in (1, 2, 3):
        for plane, rows in ((x, slice(0, TOK)), (1 - x, slice(TOK, 2 * TOK))):
            place = plane * 4 + lax.rem(y - d + 4, 4)
            k_all[place], v_all[place] = split_pair(info, mine[d - 1, rows, :], other[d - 1, rows, :])
    queries = pieces(q_ref)
    start = (jnp.full((1, HALF), -1e30, F32), jnp.zeros((ACC, HALF), F32)) * len(UNITS)
    state = lax.fori_loop(
        0, info[SEQ], lambda j, state: add_block(queries, k_all[j], v_all[j], state), start
    )
    for u in range(len(UNITS)):
        best_ref[u] = jnp.broadcast_to(state[2 * u], (8, HALF))
        acc_ref[u] = state[2 * u + 1]


def own_kernel(info, q_ref, k_ref, v_ref, best_ref, acc_ref, out_ref):
    limit = info[LENGTH] - info[SEQ] * TOK
    vt = with_ones([v_ref[i * HD : (i + 1) * HD, :] for i in range(TOK // HD)])
    queries = pieces(q_ref)
    for u, (h, i) in enumerate(UNITS):
        wide = (i + 1) * HALF
        scores = lax.dot_general(k_ref[0:wide, :], queries[u], NT, preferred_element_type=F32)
        s = lax.broadcasted_iota(jnp.int32, (wide, HALF), 0)
        t = i * HALF + lax.broadcasted_iota(jnp.int32, (wide, HALF), 1)
        keep = jnp.logical_and(s <= t, s < limit)
        scores = jnp.where(keep, scores, -jnp.inf)
        best = best_ref[u, 0:1, :]
        top = jnp.maximum(best, jnp.max(scores, axis=0, keepdims=True))
        weights = jnp.exp2((scores - top) * SCALE).astype(BF)
        shrink = jnp.exp2((best - top) * SCALE)
        summed = acc_ref[u] * shrink + jnp.dot(vt[:, 0:wide], weights, preferred_element_type=F32)
        out = summed[0:HD] * (1.0 / summed[HD : HD + 1])
        out_ref[i * HALF : (i + 1) * HALF, h * HD : (h + 1) * HD] = out.T.astype(BF)


def weights_kernel(info, near, far, out_ref, sems):
    def copies(k):
        part = pl.ds(pl.multiple_of(info[COLUMNS + k] * CB, CB), CB)
        return (
            pltpu.make_async_copy(near.at[:, part], out_ref.at[k, 0:TOK, :], sems.at[0, k]),
            pltpu.make_async_copy(far.at[:, part], out_ref.at[k, TOK : 2 * TOK, :], sems.at[1, k]),
        )

    for k in range(16):
        for copy in copies(k):
            copy.start()
    for k in range(16):
        for copy in copies(k):
            copy.wait()


def product(gated, weights, first, n):
    g = jnp.concatenate([r[...] for r in gated], axis=1)
    w = jnp.concatenate([weights[first + k] for k in range(n)], axis=1)
    return jnp.dot(g, w, preferred_element_type=F32)


def first_x_kernel(info, *refs):
    gated, weights, got, to_x, bundle = refs[0:4], refs[4], refs[5:8], refs[8], refs[9]
    for i in range(2):
        acc = product(gated, weights, 2 * i, 2).astype(BF)
        to_x[2 * i] = acc[:, 0:CB]
        to_x[2 * i + 1] = acc[:, CB : 2 * CB]
    for d in range(3):
        bundle[d] = got[d][...]


def first_z_kernel(info, *refs):
    gated, weights, to_z = refs[0:4], refs[4], refs[5:8]
    for out, d in zip(to_z, Z_ORDER):
        acc = product(gated, weights, 2 + 2 * d, 2).astype(BF)
        out[0] = acc[:, 0:CB]
        out[1] = acc[:, CB : 2 * CB]


def second_z_kernel(info, *refs):
    gated, (weights, x), to_z = refs[0:4], refs[4:6], refs[6:9]
    acc = product(gated, weights, 11, 3)
    for out, d in zip(to_z, Z_ORDER):
        part = acc[:, (d - 1) * CB : d * CB]
        out[...] = (part + x[lax.rem(info[ZPOS] + d, 4)].astype(F32)).astype(BF)


def second_x_kernel(info, *refs):
    gated, (weights, z1, z2, z3), to_x = refs[0:4], refs[4:8], refs[8:10]
    total = product(gated, weights, 10, 1)
    for r in (z1, z2, z3):
        total = total + r[1 - info[XHI]].astype(F32)
    for i in range(2):
        to_x[i][...] = total[i * HALF : (i + 1) * HALF].astype(BF)


def keep_kernel(info, *refs):
    gated, (weights, z1, z2, z3, x, out_ref) = refs[0:4], refs[4:10]
    acc = product(gated, weights, 14, 2)
    total = acc[:, 0:CB]
    for r in (z1, z2, z3):
        total = total + r[info[XHI]].astype(F32)
    out_ref[:, 0:CB] = total
    out_ref[:, CB : 2 * CB] = acc[:, CB : 2 * CB] + x[info[ZPOS]].astype(F32)


def finish_kernel(info, kept, x0, x1, z1, z2, z3, out_ref):
    for i, x in enumerate((x0, x1)):
        rows = slice(i * HALF, (i + 1) * HALF)
        out_ref[rows, 0:CB] = (kept[rows, 0:CB] + x[...].astype(F32)).astype(BF)
    total = kept[:, CB : 2 * CB]
    for r in (z1, z2, z3):
        total = total + r[...].astype(F32)
    out_ref[:, CB : 2 * CB] = total.astype(BF)


def head_perm(move):
    pairs = []
    for z in range(4):
        for x in range(2):
            for c in range(2):
                z2, x2, c2 = move(z, x, c)
                pairs.append((z * 4 + x * 2 + c, (z2 % 4) * 4 + (x2 % 2) * 2 + c2 % 2))
    return pairs


CORE_SWAP = head_perm(lambda z, x, c: (z, x, c + 1))
X_SWAP = head_perm(lambda z, x, c: (z, x + 1, c))
Z_MOVE = {d: head_perm(lambda z, x, c, d=d: (z + d, x, c)) for d in (1, 2, 3)}
LO_SWAP = [(i, (i + 4) % 8) for i in range(8)]
Y_MOVE = {d: [(x * 4 + y, x * 4 + (y + d) % 4) for x in range(2) for y in range(4)] for d in (1, 2, 3)}


def body(
    queries,
    keys,
    values,
    length,
    mixer_values,
    mixer_keys,
    mixer_queries,
    gate_values,
    step_size,
    decay_rate,
    skip_gain,
    out_weight,
):
    seq = lax.axis_index("seq")
    head = lax.axis_index("head")
    z, x, c = head // 4, (head // 2) % 2, head % 2
    block = lambda zz, xx, half: ((zz % 4) * 4 + (xx % 2) * 2 + c) * 2 + half
    columns = (
        [block(i, x + 1, 1) for i in range(4)]
        + [block(z + d, i, 0) for d in (1, 2, 3) for i in range(2)]
        + [block(z, x + 1, 0)]
        + [block(z + d, x, 1) for d in (1, 2, 3)]
        + [block(z, x, 0), block(z, x, 1)]
    )
    info = jnp.stack([seq, c, head // 2, length[0], seq % 4, seq // 4, z, x, *columns]).astype(jnp.int32)
    core = lambda a: lax.ppermute(a, "head", CORE_SWAP)
    lo = lambda a: lax.ppermute(a, "seq", LO_SWAP)
    along_y = lambda a, d: lax.ppermute(a, "seq", Y_MOVE[d])
    along_z = lambda a, d: lax.ppermute(a, "head", Z_MOVE[d])

    far_weight = core(out_weight)
    keys, values, mixer_values, mixer_keys = hbm(keys), hbm(values), hbm(mixer_values), hbm(mixer_keys)
    step_size, decay_rate, skip_gain = hbm(step_size), hbm(decay_rate), hbm(skip_gain)

    k_own, vt_own, kv, msg, cum, mv, mk = call(
        prep_kernel,
        info,
        (keys, values, mixer_values, mixer_keys, step_size, decay_rate),
        [HBM, HBM, HBM, HBM, full((HEADS, TOK)), SMEM],
        [VMEM] * 7,
        [kept_shape((TOK, HD), BF)] * 3 + [kept_shape((MSG, HD), BF), kept_shape((16, TOK), F32)] + [kept_shape((TOK, HD), BF)] * 2,
        scratch=[pltpu.VMEM((TOK, HD), BF), pltpu.SemaphoreType.DMA((4,))],
        flops=US,
    )
    from_1, from_3, from_2 = [along_y(msg, d) for d in (1, 3, 2)]
    msgs = [msg, from_1, from_2, from_3]
    kv_far = lo(kv)
    kv_far_other = core(kv_far)

    y_in = call(
        intra_kernel,
        info,
        (cum, hbm(mixer_queries), mk, mv, skip_gain),
        [VMEM, full((TOK, ROWS)), VMEM, VMEM, SMEM],
        VMEM,
        kept_shape((TOK, ROWS), F32),
        flops=US,
    )
    prefix, pdec, total, kv_pair = call(
        combine_kernel,
        info,
        (*msgs, kv, kv_far),
        [VMEM] * 6,
        [VMEM] * 4,
        [kept_shape((ROWS, HD), F32), kept_shape((8, HD), F32), kept_shape((MSG, HD), BF), kept_shape((2 * TOK, HD), BF)],
        flops=US,
        after=(y_in,),
    )
    total_far = lo(total)
    from_1, from_3, from_2 = [along_y(kv_pair, d) for d in (1, 3, 2)]
    from_y = [from_1, from_2, from_3]
    *gated, final_states = call(
        gate_kernel,
        info,
        (cum, mixer_queries, y_in, gate_values, prefix, pdec, total, total_far),
        [VMEM] * 8,
        [VMEM] * 2 + [full((HEADS, HD // 8, NST))],
        [shape((TOK, 2 * HD), BF)] * 2 + [shape((HEADS, HD // 8, NST), F32)],
        flops=US,
    )
    weights = call(
        weights_kernel,
        info,
        (hbm(out_weight), hbm(far_weight)),
        [HBM, HBM],
        VMEM,
        pltpu.VMEM((16, 2 * TOK, CB), BF),
        scratch=[pltpu.SemaphoreType.DMA((2, 16))],
        flops=10**10,
        after=(gated[0],),
    )
    gated += [core(a) for a in gated]

    to_x, bundle = call(
        first_x_kernel,
        info,
        (*gated, weights, *from_y),
        [VMEM] * 8,
        [VMEM] * 2,
        [shape((4, TOK, CB), BF), shape((3, 2 * TOK, HD), BF)],
        flops=US,
    )
    from_x = lax.ppermute(to_x, "head", X_SWAP)
    to_z = call(
        first_z_kernel,
        info,
        (*gated, weights),
        [VMEM] * 5,
        [VMEM] * 3,
        [shape((2, TOK, CB), BF)] * 3,
        flops=US,
        after=(to_x,),
    )
    from_z = [along_z(a, d) for a, d in zip(to_z, Z_ORDER)]

    best, acc = call(
        earlier_kernel,
        info,
        (queries, kv_far, kv_far_other, bundle, core(bundle)),
        [VMEM] * 5,
        [VMEM] * 2,
        [kept_shape((8, 8, HALF), F32), kept_shape((8, ACC, HALF), F32)],
        scratch=[pltpu.VMEM((8, TOK, HD), BF)] * 2,
        flops=US,
        limit=28 * 1024 * 1024,
        after=(to_z[0],),
    )

    to_z2 = call(
        second_z_kernel,
        info,
        (*gated, weights, from_x),
        [VMEM] * 6,
        [VMEM] * 3,
        [shape((TOK, CB), BF)] * 3,
        flops=US,
        after=(best,),
    )
    from_z2 = [along_z(a, d) for a, d in zip(to_z2, Z_ORDER)]
    to_x2 = call(
        second_x_kernel,
        info,
        (*gated, weights, *from_z),
        [VMEM] * 8,
        [VMEM] * 2,
        [shape((HALF, CB), BF)] * 2,
        flops=US,
        after=(to_z2[0],),
    )
    from_x2 = [lax.ppermute(a, "head", X_SWAP) for a in to_x2]
    kept = call(
        keep_kernel,
        info,
        (*gated, weights, *from_z, from_x),
        [VMEM] * 9,
        VMEM,
        shape((TOK, ROWS), F32),
        flops=US,
        after=(to_x2[0],),
    )
    attended = call(
        own_kernel,
        info,
        (queries, k_own, vt_own, best, acc),
        [VMEM] * 5,
        full((TOK, ROWS)),
        shape((TOK, ROWS), BF),
        flops=US,
        after=(kept,),
    )
    summed = call(
        finish_kernel,
        info,
        (kept, *from_x2, *from_z2),
        [VMEM] * 6,
        full((TOK, ROWS)),
        shape((TOK, ROWS), BF),
        flops=US,
        after=(hbm(attended),),
    )
    return (attended, summed, final_states)


def solution(mesh):
    placed = (
        P("seq", "head"),
        P("seq", None),
        P("seq", None),
        P(),
        P("seq", None),
        P("seq", None),
        P("seq", "head"),
        P("seq", "head"),
        P("head", "seq"),
        P("head"),
        P("head"),
        P("head", None),
    )
    return jax.shard_map(
        body,
        mesh=mesh,
        in_specs=placed,
        out_specs=(P("seq", "head"), P("seq", "head"), P("head", "seq", None)),
        check_vma=False,
    )
```

```python
import math

import jax
import jax.numpy as jnp
from jax import lax
from jax.experimental import pallas as pl
from jax.experimental.pallas import tpu as pltpu
from jax.sharding import PartitionSpec as P

H = 64
KVH = 8
HD = 128
NST = 128
TOK = 512
HEADS = 4
ROWS = HEADS * HD
MSG = ROWS + 32
CB = 256
FIRST_BLOCKS = 10
LATE_BLOCKS = 6
Z_FIRST = (2, 1, 3)
Z_SECOND = (2, 1, 3)
BF = jnp.bfloat16
F32 = jnp.float32
US = 10**5
NT = (((1,), (1,)), ((), ()))
VMEM_LIMIT = 16 * 1024 * 1024

SEQ, CORE, GROUP, LENGTH, YPOS, XLO, ZPOS, XHI, COLUMNS = range(9)


def call(kernel, info, args, in_specs, out_specs, out_shape, grid=(1,), scratch=(), flops=0, nbytes=0, trans=0, extra=(), after=(), limit=VMEM_LIMIT, alias=None):
    scalars = 1 + len(extra)
    first = scalars + len(args)

    def run(*refs):
        kernel(*refs[:first], *refs[first + len(after) :])

    aliases = {} if alias is None else {first + alias: 0}

    spec = pltpu.PrefetchScalarGridSpec(
        num_scalar_prefetch=scalars,
        grid=grid,
        in_specs=[*in_specs, *[ANY] * len(after)],
        out_specs=out_specs,
        scratch_shapes=list(scratch),
    )
    return pl.pallas_call(
        run,
        grid_spec=spec,
        out_shape=out_shape,
        input_output_aliases=aliases,
        compiler_params=pltpu.CompilerParams(vmem_limit_bytes=limit),
        cost_estimate=pl.CostEstimate(flops=flops, bytes_accessed=nbytes, transcendentals=trans),
    )(info, *extra, *args, *after)


def full(shape):
    return pl.BlockSpec(shape, lambda i, *_: (0,) * len(shape))


def hbm(a):
    return pltpu.with_memory_space_constraint(a, pltpu.HBM)


ANY = pl.BlockSpec(memory_space=pl.ANY)
HBM = pl.BlockSpec(memory_space=pltpu.HBM)
VMEM = pl.BlockSpec(memory_space=pltpu.VMEM)
SMEM = pl.BlockSpec(memory_space=pltpu.SMEM)


def shape(dims, kind):
    return jax.ShapeDtypeStruct(dims, kind)


def kept_shape(dims, kind):
    return pltpu.VMEM(dims, kind)


def split2(a):
    high = a.astype(BF)
    return high, (a - high.astype(F32)).astype(BF)


def prep_kernel(
    info, k_hbm, v_hbm, mv_hbm, mk_hbm, step_ref, rate_ref, k_ref, vt_ref, kv_ref, msg_ref, cum_ref, mv_ref, mk_ref, v_ref, sems
):
    columns = pl.ds(pl.multiple_of(info[GROUP] * HD, HD), HD)
    pairs = ((mv_hbm, mv_ref), (mk_hbm, mk_ref), (k_hbm, k_ref), (v_hbm, v_ref))
    copies = [pltpu.make_async_copy(a.at[:, columns], b, sems.at[i]) for i, (a, b) in enumerate(pairs)]
    for copy in copies:
        copy.start()

    row = lax.broadcasted_iota(jnp.int32, (8, TOK), 0)
    lane = lax.broadcasted_iota(jnp.int32, (8, TOK), 1)
    step = jnp.concatenate([step_ref[...], jnp.zeros((8 - HEADS, TOK), F32)], axis=0)
    step = jnp.where(info[SEQ] * TOK + lane < info[LENGTH], step, 0.0)
    rate = jnp.zeros((8, TOK), F32)
    for h in range(HEADS):
        rate = jnp.where(row == h, rate_ref[h], rate)
    cum = -step * rate
    shift = 1
    while shift < TOK:
        cum = cum + jnp.where(lane >= shift, pltpu.roll(cum, shift, 1), 0.0)
        shift *= 2
    cum_ref[0:8, :] = cum
    cum_ref[8:16, :] = step
    last = cum[:, TOK - 1 : TOK]
    tail = jnp.exp(last - cum) * step
    log = jnp.broadcast_to(last, (8, HD))
    high = log.astype(BF).astype(F32)
    mid = (log - high).astype(BF).astype(F32)
    low = log - high - mid
    msg_ref[ROWS:MSG, :] = jnp.concatenate([high, mid, low, jnp.zeros_like(low)], axis=0).astype(BF)
    copies[0].wait()
    copies[1].wait()
    vt = mv_ref[...].astype(F32).T
    mk = mk_ref[...]
    for h in range(HEADS):
        high, low = split2(vt * tail[h : h + 1, :])
        state = jnp.dot(high, mk, preferred_element_type=F32) + jnp.dot(low, mk, preferred_element_type=F32)
        msg_ref[h * HD : (h + 1) * HD, :] = state.astype(BF)
    copies[2].wait()
    copies[3].wait()
    zero = info[CORE] == 0
    for i in range(TOK // HD):
        part = pl.ds(i * HD, HD)
        turned = v_ref[part, :].astype(F32).T
        vt_ref[part, :] = turned.astype(BF)
        kv_ref[part, :] = jnp.where(zero, k_ref[part, :].astype(F32), turned).astype(BF)


def log_of(msg):
    tail = msg[ROWS:MSG, :].astype(F32)
    return tail[0:8] + tail[8:16] + tail[16:24]


def combine_kernel(info, m0, m1, m2, m3, kv, kv_far, prefix_ref, pdec_ref, total_ref, pair_ref):
    pair_ref[0:TOK, :] = kv[...]
    pair_ref[TOK : 2 * TOK, :] = kv_far[...]
    y = info[YPOS]
    msgs = (m0, m1, m2, m3)
    place = [lax.rem(y - d + 4, 4) for d in range(4)]
    logs = [log_of(m) for m in msgs]
    pre, tot = [], []
    for d in range(4):
        in_pre = jnp.zeros_like(logs[0])
        in_tot = jnp.zeros_like(logs[0])
        for e in range(4):
            if e == d:
                continue
            after = place[e] > place[d]
            in_tot = in_tot + jnp.where(after, logs[e], 0.0)
            in_pre = in_pre + jnp.where(jnp.logical_and(after, place[e] < y), logs[e], 0.0)
        tot.append(jnp.exp(in_tot))
        pre.append(jnp.where(place[d] < y, jnp.exp(in_pre), 0.0))
    whole = logs[0] + logs[1] + logs[2] + logs[3]
    before = jnp.zeros_like(whole)
    for e in range(4):
        before = before + jnp.where(place[e] < y, logs[e], 0.0)
    pdec_ref[...] = jnp.exp(before)
    for h in range(HEADS):
        part = slice(h * HD, (h + 1) * HD)
        own = [m[part, :].astype(F32) for m in msgs]
        total = own[0] * tot[0][h : h + 1]
        prefix = own[1] * pre[1][h : h + 1]
        for d in range(1, 4):
            total = total + own[d] * tot[d][h : h + 1]
        for d in range(2, 4):
            prefix = prefix + own[d] * pre[d][h : h + 1]
        prefix_ref[part, :] = prefix
        total_ref[part, :] = total.astype(BF)
    high = whole.astype(BF).astype(F32)
    mid = (whole - high).astype(BF).astype(F32)
    low = whole - high - mid
    total_ref[ROWS:MSG, :] = jnp.concatenate([high, mid, low, jnp.zeros_like(low)], axis=0).astype(BF)


def intra_kernel(info, cum_ref, c_ref, mk_ref, mv_ref, skip_ref, y_ref):
    cum = cum_ref[0:8, :]
    step = cum_ref[8:16, :]
    cols = cum.T
    half = TOK // 2
    for h in range(HEADS):
        part = slice(h * HD, (h + 1) * HD)
        for i in range(2):
            here = slice(i * half, (i + 1) * half)
            wide = (i + 1) * half
            inner = lax.dot_general(c_ref[here, part], mk_ref[0:wide, :], NT, preferred_element_type=F32)
            t = i * half + lax.broadcasted_iota(jnp.int32, (half, wide), 0)
            s = lax.broadcasted_iota(jnp.int32, (half, wide), 1)
            diff = jnp.where(s <= t, cols[here, h : h + 1] - cum[h : h + 1, 0:wide], -jnp.inf)
            mix = (jnp.exp(diff) * inner * step[h : h + 1, 0:wide]).astype(BF)
            y = jnp.dot(mix, mv_ref[0:wide, :], preferred_element_type=F32)
            y_ref[here, part] = y + skip_ref[h] * mv_ref[here, :].astype(F32)


def gate_kernel(info, cum_ref, c_ref, y_ref, g_ref, prefix_ref, pdec_ref, own_ref, got_ref, out0, out1, fin_ref):
    second = info[XLO] == 1
    ecols = jnp.exp(cum_ref[0:8, :]).T
    for h in range(HEADS):
        part = slice(h * HD, (h + 1) * HD)
        far = pdec_ref[h : h + 1, :] * got_ref[part, :].astype(F32)
        state = prefix_ref[part, :] + jnp.where(second, far, 0.0)
        high, low = split2(state)
        c = c_ref[:, part]
        carried = lax.dot_general(
            jnp.concatenate([c, c], axis=1), jnp.concatenate([high, low], axis=1), NT, preferred_element_type=F32
        )
        y = y_ref[:, part] + ecols[:, h : h + 1] * carried
        g = g_ref[:, part].astype(F32)
        (out0, out1)[h // 2][:, (h % 2) * HD : (h % 2 + 1) * HD] = (y * (g / (1.0 + jnp.exp(-g)))).astype(BF)
    own_log = log_of(own_ref)
    got_log = log_of(got_ref)
    later = jnp.exp(jnp.where(second, own_log, got_log))
    for h in range(HEADS):
        rows = pl.ds(pl.multiple_of(h * HD + info[SEQ] * (HD // 8), HD // 8), HD // 8)
        own = own_ref[rows, :].astype(F32)
        got = got_ref[rows, :].astype(F32)
        first = jnp.where(second, got, own)
        last = jnp.where(second, own, got)
        fin_ref[h] = last + later[h : h + 1, :] * first


SCALE = math.log2(math.e) / math.sqrt(HD)
HALF = TOK // 2
UNITS = [(h, i) for h in range(HEADS) for i in range(2)]
ACC = HD + 16


def with_ones(panels):
    vt = jnp.concatenate(panels, axis=1)
    return jnp.concatenate([vt, jnp.ones((16, vt.shape[1]), BF)], axis=0)


def split_pair(info, mine, other):
    zero = jnp.broadcast_to(info[CORE], mine.shape) == 0
    a, b = mine.astype(F32), other.astype(F32)
    return jnp.where(zero, a, b).astype(BF), jnp.where(zero, b, a).astype(BF)


def pieces(q_ref):
    return [q_ref[i * HALF : (i + 1) * HALF, h * HD : (h + 1) * HD] for h, i in UNITS]


def add_block(queries, k, v, state):
    vt = with_ones([v[i * HD : (i + 1) * HD] for i in range(TOK // HD)])
    scores = [lax.dot_general(k, q, NT, preferred_element_type=F32) for q in queries]
    new = []
    for u in range(len(UNITS)):
        best, summed = state[2 * u], state[2 * u + 1]
        top = jnp.maximum(best, jnp.max(scores[u], axis=0, keepdims=True))
        weights = jnp.exp2((scores[u] - top) * SCALE).astype(BF)
        shrink = jnp.exp2((best - top) * SCALE)
        new += [top, summed * shrink + jnp.dot(vt, weights, preferred_element_type=F32)]
    return tuple(new)


def attend_kernel(
    info, q_ref, k_ref, v_ref, far, far_other, mine, other, g0, g1, g2, g3, near_w, far_w,
    out_ref, late_ref, ready_ref, k_all, v_all, sems,
):
    copies = weight_copies(info, near_w, far_w, late_ref, sems, FIRST_BLOCKS, LATE_BLOCKS)
    for copy in copies:
        copy.start()
    y, x = info[YPOS], info[XLO]
    place = (1 - x) * 4 + y
    k_all[place], v_all[place] = split_pair(info, far[...], far_other[...])
    for d in (1, 2, 3):
        for plane, rows in ((x, slice(0, TOK)), (1 - x, slice(TOK, 2 * TOK))):
            place = plane * 4 + lax.rem(y - d + 4, 4)
            k_all[place], v_all[place] = split_pair(info, mine[d - 1, rows, :], other[d - 1, rows, :])
    limit = info[LENGTH] - info[SEQ] * TOK
    vt = with_ones([v_ref[i * HD : (i + 1) * HD, :] for i in range(TOK // HD)])
    queries = pieces(q_ref)
    state = []
    for u, (h, i) in enumerate(UNITS):
        wide = (i + 1) * HALF
        scores = lax.dot_general(k_ref[0:wide, :], queries[u], NT, preferred_element_type=F32)
        s = lax.broadcasted_iota(jnp.int32, (wide, HALF), 0)
        t = i * HALF + lax.broadcasted_iota(jnp.int32, (wide, HALF), 1)
        keep = jnp.logical_and(s <= t, s < limit)
        scores = jnp.where(keep, scores, -jnp.inf)
        best = jnp.max(scores, axis=0, keepdims=True)
        weights = jnp.exp2((scores - best) * SCALE).astype(BF)
        state += [best, jnp.dot(vt[:, 0:wide], weights, preferred_element_type=F32)]
    state = lax.fori_loop(
        0, info[SEQ], lambda j, state: add_block(queries, k_all[j], v_all[j], state), tuple(state)
    )
    for u, (h, i) in enumerate(UNITS):
        summed = state[2 * u + 1]
        out = summed[0:HD] * (1.0 / summed[HD : HD + 1])
        out_ref[i * HALF : (i + 1) * HALF, h * HD : (h + 1) * HD] = out.T.astype(BF)
    for copy in copies:
        copy.wait()
    for i in range(2):
        acc = product((g0, g1, g2, g3), late_ref, 2 * i, 2)
        ready_ref[2 * i] = acc[:, 0:CB]
        ready_ref[2 * i + 1] = acc[:, CB : 2 * CB]


def weight_copies(info, near, far, out_ref, sems, first, n):
    copies = []
    for k in range(n):
        part = pl.ds(pl.multiple_of(info[COLUMNS + first + k] * CB, CB), CB)
        copies += [
            pltpu.make_async_copy(near.at[:, part], out_ref.at[k, 0:TOK, :], sems.at[0, k]),
            pltpu.make_async_copy(far.at[:, part], out_ref.at[k, TOK : 2 * TOK, :], sems.at[1, k]),
        ]
    return copies


def weights_kernel(info, near, far, out_ref, sems):
    copies = weight_copies(info, near, far, out_ref, sems, 0, FIRST_BLOCKS)
    for copy in copies:
        copy.start()
    for copy in copies:
        copy.wait()


def product(gated, weights, first, n):
    g = jnp.concatenate([r[...] for r in gated], axis=1)
    w = jnp.concatenate([weights[first + k] for k in range(n)], axis=1)
    return jnp.dot(g, w, preferred_element_type=F32)


def first_kernel(info, *refs):
    gated, weights, to_x, to_z = refs[0:4], refs[4], refs[5], refs[6:9]
    for i in range(2):
        acc = product(gated, weights, 2 * i, 2).astype(BF)
        to_x[2 * i] = acc[:, 0:CB]
        to_x[2 * i + 1] = acc[:, CB : 2 * CB]
    for out, d in zip(to_z, Z_FIRST):
        acc = product(gated, weights, 2 + 2 * d, 2).astype(BF)
        out[0] = acc[:, 0:CB]
        out[1] = acc[:, CB : 2 * CB]


def bundle_kernel(info, y1, y2, y3, same_ref, bundle_ref):
    for d, r in enumerate((y1, y2, y3)):
        bundle_ref[d] = r[...]


def second_z_kernel(info, ready, x, *to_z):
    for out, d in zip(to_z, Z_SECOND):
        out[...] = (ready[d] + x[lax.rem(info[ZPOS] + d, 4)].astype(F32)).astype(BF)


def second_x_kernel(info, ready, z1, z2, z3, to_x):
    total = ready[0]
    for r in (z1, z2, z3):
        total = total + r[1 - info[XHI]].astype(F32)
    to_x[...] = total.astype(BF)


def keep_kernel(info, *refs):
    gated, (weights, z1, z2, z3, x, out_ref) = refs[0:4], refs[4:10]
    acc = product(gated, weights, 4, 2)
    total = acc[:, 0:CB]
    for r in (z1, z2, z3):
        total = total + r[info[XHI]].astype(F32)
    out_ref[:, 0:CB] = total
    out_ref[:, CB : 2 * CB] = acc[:, CB : 2 * CB] + x[info[ZPOS]].astype(F32)


def finish_kernel(info, kept, x, z1, z2, z3, out_ref):
    out_ref[:, 0:CB] = (kept[:, 0:CB] + x[...].astype(F32)).astype(BF)
    total = kept[:, CB : 2 * CB]
    for r in (z1, z2, z3):
        total = total + r[...].astype(F32)
    out_ref[:, CB : 2 * CB] = total.astype(BF)


def head_perm(move):
    pairs = []
    for z in range(4):
        for x in range(2):
            for c in range(2):
                z2, x2, c2 = move(z, x, c)
                pairs.append((z * 4 + x * 2 + c, (z2 % 4) * 4 + (x2 % 2) * 2 + c2 % 2))
    return pairs


CORE_SWAP = head_perm(lambda z, x, c: (z, x, c + 1))
X_SWAP = head_perm(lambda z, x, c: (z, x + 1, c))
Z_MOVE = {d: head_perm(lambda z, x, c, d=d: (z + d, x, c)) for d in (1, 2, 3)}
LO_SWAP = [(i, (i + 4) % 8) for i in range(8)]
Y_MOVE = {d: [(x * 4 + y, x * 4 + (y + d) % 4) for x in range(2) for y in range(4)] for d in (1, 2, 3)}


def body(
    queries,
    keys,
    values,
    length,
    mixer_values,
    mixer_keys,
    mixer_queries,
    gate_values,
    step_size,
    decay_rate,
    skip_gain,
    out_weight,
):
    seq = lax.axis_index("seq")
    head = lax.axis_index("head")
    z, x, c = head // 4, (head // 2) % 2, head % 2
    block = lambda zz, xx, half: ((zz % 4) * 4 + (xx % 2) * 2 + c) * 2 + half
    columns = (
        [block(i, x + 1, 1) for i in range(4)]
        + [block(z + d, i, 0) for d in (1, 2, 3) for i in range(2)]
        + [block(z, x + 1, 0)]
        + [block(z + d, x, 1) for d in (1, 2, 3)]
        + [block(z, x, 0), block(z, x, 1)]
    )
    info = jnp.stack([seq, c, head // 2, length[0], seq % 4, seq // 4, z, x, *columns]).astype(jnp.int32)
    core = lambda a: lax.ppermute(a, "head", CORE_SWAP)
    lo = lambda a: lax.ppermute(a, "seq", LO_SWAP)
    along_y = lambda a, d: lax.ppermute(a, "seq", Y_MOVE[d])
    along_z = lambda a, d: lax.ppermute(a, "head", Z_MOVE[d])

    far_weight = core(out_weight)
    keys, values, mixer_values, mixer_keys = hbm(keys), hbm(values), hbm(mixer_values), hbm(mixer_keys)
    step_size, decay_rate, skip_gain = hbm(step_size), hbm(decay_rate), hbm(skip_gain)

    k_own, vt_own, kv, msg, cum, mv, mk = call(
        prep_kernel,
        info,
        (keys, values, mixer_values, mixer_keys, step_size, decay_rate),
        [HBM, HBM, HBM, HBM, full((HEADS, TOK)), SMEM],
        [VMEM] * 7,
        [kept_shape((TOK, HD), BF)] * 3 + [kept_shape((MSG, HD), BF), kept_shape((16, TOK), F32)] + [kept_shape((TOK, HD), BF)] * 2,
        scratch=[pltpu.VMEM((TOK, HD), BF), pltpu.SemaphoreType.DMA((4,))],
        flops=US,
    )
    from_1, from_3, from_2 = [along_y(msg, d) for d in (1, 3, 2)]
    msgs = [msg, from_1, from_2, from_3]
    kv_far = lo(kv)
    kv_far_other = core(kv_far)

    y_in = call(
        intra_kernel,
        info,
        (cum, hbm(mixer_queries), mk, mv, skip_gain),
        [VMEM, full((TOK, ROWS)), VMEM, VMEM, SMEM],
        VMEM,
        kept_shape((TOK, ROWS), F32),
        flops=US,
    )
    prefix, pdec, total, kv_pair = call(
        combine_kernel,
        info,
        (*msgs, kv, kv_far),
        [VMEM] * 6,
        [VMEM] * 4,
        [kept_shape((ROWS, HD), F32), kept_shape((8, HD), F32), kept_shape((MSG, HD), BF), kept_shape((2 * TOK, HD), BF)],
        flops=US,
        after=(y_in,),
    )
    total_far = lo(total)
    from_1, from_3, from_2 = [along_y(kv_pair, d) for d in (1, 3, 2)]
    from_y = [from_1, from_2, from_3]
    *gated, final_states = call(
        gate_kernel,
        info,
        (cum, mixer_queries, y_in, gate_values, prefix, pdec, total, total_far),
        [VMEM] * 8,
        [VMEM] * 2 + [full((HEADS, HD // 8, NST))],
        [shape((TOK, 2 * HD), BF)] * 2 + [shape((HEADS, HD // 8, NST), F32)],
        flops=US,
    )
    weights = call(
        weights_kernel,
        info,
        (hbm(out_weight), hbm(far_weight)),
        [HBM, HBM],
        VMEM,
        kept_shape((FIRST_BLOCKS, 2 * TOK, CB), BF),
        scratch=[pltpu.SemaphoreType.DMA((2, FIRST_BLOCKS))],
        flops=10**10,
        after=(gated[0],),
    )
    gated += [core(a) for a in gated]

    to_x, *to_z = call(
        first_kernel,
        info,
        (*gated, weights),
        [VMEM] * 5,
        [VMEM] * 4,
        [kept_shape((4, TOK, CB), BF)] + [kept_shape((2, TOK, CB), BF)] * 3,
        flops=US,
    )
    to_x, bundle = call(
        bundle_kernel,
        info,
        from_y,
        [VMEM] * 3,
        [ANY, VMEM],
        [kept_shape((4, TOK, CB), BF), kept_shape((3, 2 * TOK, HD), BF)],
        flops=US,
        after=(to_x,),
        alias=0,
    )
    from_x = lax.ppermute(to_x, "head", X_SWAP)
    from_z = [along_z(a, d) for a, d in zip(to_z, Z_FIRST)]

    attended, late, ready = call(
        attend_kernel,
        info,
        (queries, k_own, vt_own, kv_far, kv_far_other, bundle, core(bundle), *gated, hbm(out_weight), hbm(far_weight)),
        [VMEM] * 11 + [HBM] * 2,
        [full((TOK, ROWS)), VMEM, VMEM],
        [shape((TOK, ROWS), BF), kept_shape((LATE_BLOCKS, 2 * TOK, CB), BF), kept_shape((4, TOK, CB), F32)],
        scratch=[pltpu.VMEM((8, TOK, HD), BF)] * 2 + [pltpu.SemaphoreType.DMA((2, LATE_BLOCKS))],
        flops=US,
        limit=28 * 1024 * 1024,
        after=(to_z[0],),
    )
    to_z2 = call(
        second_z_kernel,
        info,
        (ready, from_x),
        [VMEM] * 2,
        [VMEM] * 3,
        [shape((TOK, CB), BF)] * 3,
        flops=US,
    )
    from_z2 = [along_z(a, d) for a, d in zip(to_z2, Z_SECOND)]
    to_x2 = call(
        second_x_kernel,
        info,
        (ready, *from_z),
        [VMEM] * 4,
        VMEM,
        shape((TOK, CB), BF),
        flops=US,
        after=(to_z2[0],),
    )
    from_x2 = lax.ppermute(to_x2, "head", X_SWAP)
    kept = call(
        keep_kernel,
        info,
        (*gated, late, *from_z, from_x),
        [VMEM] * 9,
        VMEM,
        shape((TOK, ROWS), F32),
        flops=US,
        after=(to_x2,),
    )
    summed = call(
        finish_kernel,
        info,
        (kept, from_x2, *from_z2),
        [VMEM] * 5,
        full((TOK, ROWS)),
        shape((TOK, ROWS), BF),
        flops=US,
    )
    return (attended, summed, final_states)


def solution(mesh):
    placed = (
        P("seq", "head"),
        P("seq", None),
        P("seq", None),
        P(),
        P("seq", None),
        P("seq", None),
        P("seq", "head"),
        P("seq", "head"),
        P("head", "seq"),
        P("head"),
        P("head"),
        P("head", None),
    )
    return jax.shard_map(
        body,
        mesh=mesh,
        in_specs=placed,
        out_specs=(P("seq", "head"), P("seq", "head"), P("head", "seq", None)),
        check_vma=False,
    )
```

```python
import math

import jax
import jax.numpy as jnp
from jax import lax
from jax.experimental import pallas as pl
from jax.experimental.pallas import tpu as pltpu
from jax.sharding import PartitionSpec as P

H = 64
KVH = 8
HD = 128
NST = 128
TOK = 512
HEADS = 4
ROWS = HEADS * HD
MSG = ROWS + 32
CB = 256
FIRST_BLOCKS = 10
LATE_BLOCKS = 6
Z_FIRST = (2, 1, 3)
Z_SECOND = (2, 1, 3)
BF = jnp.bfloat16
F32 = jnp.float32
US = 10**5
NT = (((1,), (1,)), ((), ()))
VMEM_LIMIT = 16 * 1024 * 1024

SEQ, CORE, GROUP, LENGTH, YPOS, XLO, ZPOS, XHI, COLUMNS = range(9)


def call(kernel, info, args, in_specs, out_specs, out_shape, grid=(1,), scratch=(), flops=0, nbytes=0, trans=0, extra=(), after=(), limit=VMEM_LIMIT, alias=None):
    scalars = 1 + len(extra)
    first = scalars + len(args)

    def run(*refs):
        kernel(*refs[:first], *refs[first + len(after) :])

    aliases = {} if alias is None else {first + alias: 0}

    spec = pltpu.PrefetchScalarGridSpec(
        num_scalar_prefetch=scalars,
        grid=grid,
        in_specs=[*in_specs, *[ANY] * len(after)],
        out_specs=out_specs,
        scratch_shapes=list(scratch),
    )
    return pl.pallas_call(
        run,
        grid_spec=spec,
        out_shape=out_shape,
        input_output_aliases=aliases,
        compiler_params=pltpu.CompilerParams(vmem_limit_bytes=limit),
        cost_estimate=pl.CostEstimate(flops=flops, bytes_accessed=nbytes, transcendentals=trans),
    )(info, *extra, *args, *after)


def full(shape):
    return pl.BlockSpec(shape, lambda i, *_: (0,) * len(shape))


def hbm(a):
    return pltpu.with_memory_space_constraint(a, pltpu.HBM)


ANY = pl.BlockSpec(memory_space=pl.ANY)
HBM = pl.BlockSpec(memory_space=pltpu.HBM)
VMEM = pl.BlockSpec(memory_space=pltpu.VMEM)
SMEM = pl.BlockSpec(memory_space=pltpu.SMEM)


def shape(dims, kind):
    return jax.ShapeDtypeStruct(dims, kind)


def kept_shape(dims, kind):
    return pltpu.VMEM(dims, kind)


def split2(a):
    high = a.astype(BF)
    return high, (a - high.astype(F32)).astype(BF)


def prep_kernel(
    info, k_hbm, v_hbm, mv_hbm, mk_hbm, step_ref, rate_ref, k_ref, vt_ref, kv_ref, msg_ref, cum_ref, mv_ref, mk_ref, v_ref, sems
):
    columns = pl.ds(pl.multiple_of(info[GROUP] * HD, HD), HD)
    pairs = ((mv_hbm, mv_ref), (mk_hbm, mk_ref), (k_hbm, k_ref), (v_hbm, v_ref))
    copies = [pltpu.make_async_copy(a.at[:, columns], b, sems.at[i]) for i, (a, b) in enumerate(pairs)]
    for copy in copies:
        copy.start()

    row = lax.broadcasted_iota(jnp.int32, (8, TOK), 0)
    lane = lax.broadcasted_iota(jnp.int32, (8, TOK), 1)
    step = jnp.concatenate([step_ref[...], jnp.zeros((8 - HEADS, TOK), F32)], axis=0)
    step = jnp.where(info[SEQ] * TOK + lane < info[LENGTH], step, 0.0)
    rate = jnp.zeros((8, TOK), F32)
    for h in range(HEADS):
        rate = jnp.where(row == h, rate_ref[h], rate)
    cum = -step * rate
    shift = 1
    while shift < TOK:
        cum = cum + jnp.where(lane >= shift, pltpu.roll(cum, shift, 1), 0.0)
        shift *= 2
    cum_ref[0:8, :] = cum
    cum_ref[8:16, :] = step
    last = cum[:, TOK - 1 : TOK]
    tail = jnp.exp(last - cum) * step
    log = jnp.broadcast_to(last, (8, HD))
    high = log.astype(BF).astype(F32)
    mid = (log - high).astype(BF).astype(F32)
    low = log - high - mid
    msg_ref[ROWS:MSG, :] = jnp.concatenate([high, mid, low, jnp.zeros_like(low)], axis=0).astype(BF)
    copies[0].wait()
    copies[1].wait()
    vt = mv_ref[...].astype(F32).T
    mk = mk_ref[...]
    for h in range(HEADS):
        high, low = split2(vt * tail[h : h + 1, :])
        state = jnp.dot(high, mk, preferred_element_type=F32) + jnp.dot(low, mk, preferred_element_type=F32)
        msg_ref[h * HD : (h + 1) * HD, :] = state.astype(BF)
    copies[2].wait()
    copies[3].wait()
    zero = info[CORE] == 0
    for i in range(TOK // HD):
        part = pl.ds(i * HD, HD)
        turned = v_ref[part, :].astype(F32).T
        vt_ref[part, :] = turned.astype(BF)
        kv_ref[part, :] = jnp.where(zero, k_ref[part, :].astype(F32), turned).astype(BF)


def log_of(msg):
    tail = msg[ROWS:MSG, :].astype(F32)
    return tail[0:8] + tail[8:16] + tail[16:24]


def combine_kernel(info, m0, m1, m2, m3, kv, kv_far, prefix_ref, pdec_ref, total_ref, pair_ref):
    pair_ref[0:TOK, :] = kv[...]
    pair_ref[TOK : 2 * TOK, :] = kv_far[...]
    y = info[YPOS]
    msgs = (m0, m1, m2, m3)
    place = [lax.rem(y - d + 4, 4) for d in range(4)]
    logs = [log_of(m) for m in msgs]
    pre, tot = [], []
    for d in range(4):
        in_pre = jnp.zeros_like(logs[0])
        in_tot = jnp.zeros_like(logs[0])
        for e in range(4):
            if e == d:
                continue
            after = place[e] > place[d]
            in_tot = in_tot + jnp.where(after, logs[e], 0.0)
            in_pre = in_pre + jnp.where(jnp.logical_and(after, place[e] < y), logs[e], 0.0)
        tot.append(jnp.exp(in_tot))
        pre.append(jnp.where(place[d] < y, jnp.exp(in_pre), 0.0))
    whole = logs[0] + logs[1] + logs[2] + logs[3]
    before = jnp.zeros_like(whole)
    for e in range(4):
        before = before + jnp.where(place[e] < y, logs[e], 0.0)
    pdec_ref[...] = jnp.exp(before)
    for h in range(HEADS):
        part = slice(h * HD, (h + 1) * HD)
        own = [m[part, :].astype(F32) for m in msgs]
        total = own[0] * tot[0][h : h + 1]
        prefix = own[1] * pre[1][h : h + 1]
        for d in range(1, 4):
            total = total + own[d] * tot[d][h : h + 1]
        for d in range(2, 4):
            prefix = prefix + own[d] * pre[d][h : h + 1]
        prefix_ref[part, :] = prefix
        total_ref[part, :] = total.astype(BF)
    high = whole.astype(BF).astype(F32)
    mid = (whole - high).astype(BF).astype(F32)
    low = whole - high - mid
    total_ref[ROWS:MSG, :] = jnp.concatenate([high, mid, low, jnp.zeros_like(low)], axis=0).astype(BF)


def intra_kernel(info, cum_ref, c_ref, mk_ref, mv_ref, skip_ref, y_ref):
    cum = cum_ref[0:8, :]
    step = cum_ref[8:16, :]
    cols = cum.T
    half = TOK // 2
    for h in range(HEADS):
        part = slice(h * HD, (h + 1) * HD)
        for i in range(2):
            here = slice(i * half, (i + 1) * half)
            wide = (i + 1) * half
            inner = lax.dot_general(c_ref[here, part], mk_ref[0:wide, :], NT, preferred_element_type=F32)
            t = i * half + lax.broadcasted_iota(jnp.int32, (half, wide), 0)
            s = lax.broadcasted_iota(jnp.int32, (half, wide), 1)
            diff = jnp.where(s <= t, cols[here, h : h + 1] - cum[h : h + 1, 0:wide], -jnp.inf)
            mix = (jnp.exp(diff) * inner * step[h : h + 1, 0:wide]).astype(BF)
            y = jnp.dot(mix, mv_ref[0:wide, :], preferred_element_type=F32)
            y_ref[here, part] = y + skip_ref[h] * mv_ref[here, :].astype(F32)


def gate_kernel(info, cum_ref, c_ref, y_ref, g_ref, prefix_ref, pdec_ref, own_ref, got_ref, out0, out1, fin_ref):
    second = info[XLO] == 1
    ecols = jnp.exp(cum_ref[0:8, :]).T
    for h in range(HEADS):
        part = slice(h * HD, (h + 1) * HD)
        far = pdec_ref[h : h + 1, :] * got_ref[part, :].astype(F32)
        state = prefix_ref[part, :] + jnp.where(second, far, 0.0)
        high, low = split2(state)
        c = c_ref[:, part]
        carried = lax.dot_general(
            jnp.concatenate([c, c], axis=1), jnp.concatenate([high, low], axis=1), NT, preferred_element_type=F32
        )
        y = y_ref[:, part] + ecols[:, h : h + 1] * carried
        g = g_ref[:, part].astype(F32)
        (out0, out1)[h // 2][:, (h % 2) * HD : (h % 2 + 1) * HD] = (y * (g / (1.0 + jnp.exp(-g)))).astype(BF)
    own_log = log_of(own_ref)
    got_log = log_of(got_ref)
    later = jnp.exp(jnp.where(second, own_log, got_log))
    for h in range(HEADS):
        rows = pl.ds(pl.multiple_of(h * HD + info[SEQ] * (HD // 8), HD // 8), HD // 8)
        own = own_ref[rows, :].astype(F32)
        got = got_ref[rows, :].astype(F32)
        first = jnp.where(second, got, own)
        last = jnp.where(second, own, got)
        fin_ref[h] = last + later[h : h + 1, :] * first


SCALE = math.log2(math.e) / math.sqrt(HD)
HALF = TOK // 2
UNITS = [(h, i) for h in range(HEADS) for i in range(2)]
ACC = HD + 16


def with_ones(panels):
    vt = jnp.concatenate(panels, axis=1)
    return jnp.concatenate([vt, jnp.ones((16, vt.shape[1]), BF)], axis=0)


def split_pair(info, mine, other):
    zero = jnp.broadcast_to(info[CORE], mine.shape) == 0
    a, b = mine.astype(F32), other.astype(F32)
    return jnp.where(zero, a, b).astype(BF), jnp.where(zero, b, a).astype(BF)


def pieces(q_ref):
    return [q_ref[i * HALF : (i + 1) * HALF, h * HD : (h + 1) * HD] for h, i in UNITS]


def add_block(queries, k, v, state):
    vt = with_ones([v[i * HD : (i + 1) * HD] for i in range(TOK // HD)])
    scores = [lax.dot_general(k, q, NT, preferred_element_type=F32) for q in queries]
    new = []
    for u in range(len(UNITS)):
        best, summed = state[2 * u], state[2 * u + 1]
        top = jnp.maximum(best, jnp.max(scores[u], axis=0, keepdims=True))
        weights = jnp.exp2((scores[u] - top) * SCALE).astype(BF)
        shrink = jnp.exp2((best - top) * SCALE)
        new += [top, summed * shrink + jnp.dot(vt, weights, preferred_element_type=F32)]
    return tuple(new)


def attend_kernel(
    info, q_ref, k_ref, v_ref, far, far_other, mine, other, g0, g1, g2, g3, near_w, far_w,
    out_ref, late_ref, ready_ref, k_all, v_all, sems,
):
    copies = weight_copies(info, near_w, far_w, late_ref, sems, FIRST_BLOCKS, LATE_BLOCKS)
    for copy in copies:
        copy.start()
    y, x = info[YPOS], info[XLO]
    place = (1 - x) * 4 + y
    k_all[place], v_all[place] = split_pair(info, far[...], far_other[...])
    for d in (1, 2, 3):
        for plane, rows in ((x, slice(0, TOK)), (1 - x, slice(TOK, 2 * TOK))):
            place = plane * 4 + lax.rem(y - d + 4, 4)
            k_all[place], v_all[place] = split_pair(info, mine[d - 1, rows, :], other[d - 1, rows, :])
    limit = info[LENGTH] - info[SEQ] * TOK
    vt = with_ones([v_ref[i * HD : (i + 1) * HD, :] for i in range(TOK // HD)])
    queries = pieces(q_ref)
    state = []
    for u, (h, i) in enumerate(UNITS):
        wide = (i + 1) * HALF
        scores = lax.dot_general(k_ref[0:wide, :], queries[u], NT, preferred_element_type=F32)
        s = lax.broadcasted_iota(jnp.int32, (wide, HALF), 0)
        t = i * HALF + lax.broadcasted_iota(jnp.int32, (wide, HALF), 1)
        keep = jnp.logical_and(s <= t, s < limit)
        scores = jnp.where(keep, scores, -jnp.inf)
        best = jnp.max(scores, axis=0, keepdims=True)
        weights = jnp.exp2((scores - best) * SCALE).astype(BF)
        state += [best, jnp.dot(vt[:, 0:wide], weights, preferred_element_type=F32)]
    state = lax.fori_loop(
        0, info[SEQ], lambda j, state: add_block(queries, k_all[j], v_all[j], state), tuple(state)
    )
    for u, (h, i) in enumerate(UNITS):
        summed = state[2 * u + 1]
        out = summed[0:HD] * (1.0 / summed[HD : HD + 1])
        out_ref[i * HALF : (i + 1) * HALF, h * HD : (h + 1) * HD] = out.T.astype(BF)
    for copy in copies:
        copy.wait()
    for i in range(2):
        acc = product((g0, g1, g2, g3), late_ref, 2 * i, 2)
        ready_ref[2 * i] = acc[:, 0:CB]
        ready_ref[2 * i + 1] = acc[:, CB : 2 * CB]


def weight_copies(info, near, far, out_ref, sems, first, n):
    copies = []
    for k in range(n):
        part = pl.ds(pl.multiple_of(info[COLUMNS + first + k] * CB, CB), CB)
        copies += [
            pltpu.make_async_copy(near.at[:, part], out_ref.at[k, 0:TOK, :], sems.at[0, k]),
            pltpu.make_async_copy(far.at[:, part], out_ref.at[k, TOK : 2 * TOK, :], sems.at[1, k]),
        ]
    return copies


def weights_kernel(info, near, far, out_ref, sems):
    copies = weight_copies(info, near, far, out_ref, sems, 0, FIRST_BLOCKS)
    for copy in copies:
        copy.start()
    for copy in copies:
        copy.wait()


def product(gated, weights, first, n):
    g = jnp.concatenate([r[...] for r in gated], axis=1)
    w = jnp.concatenate([weights[first + k] for k in range(n)], axis=1)
    return jnp.dot(g, w, preferred_element_type=F32)


def first_kernel(info, *refs):
    gated, weights, to_x, to_z = refs[0:4], refs[4], refs[5:7], refs[7:10]
    for i in range(2):
        acc = product(gated, weights, 2 * i, 2).astype(BF)
        to_x[i][0] = acc[:, 0:CB]
        to_x[i][1] = acc[:, CB : 2 * CB]
    for out, d in zip(to_z, Z_FIRST):
        acc = product(gated, weights, 2 + 2 * d, 2).astype(BF)
        out[0] = acc[:, 0:CB]
        out[1] = acc[:, CB : 2 * CB]


def bundle_kernel(info, y1, y2, y3, same_ref, bundle_ref):
    for d, r in enumerate((y1, y2, y3)):
        bundle_ref[d] = r[...]


def second_even_kernel(info, ready, x, to_z):
    to_z[0:TOK, :] = (ready[2] + x[1].astype(F32)).astype(BF)
    to_z[TOK:, :] = jnp.zeros((32, CB), BF)


def second_odd_kernel(info, ready, x, *to_z):
    for i, d in enumerate((1, 3)):
        to_z[i][...] = (ready[d] + x[i].astype(F32)).astype(BF)


def second_x_kernel(info, ready, z1, z2, z3, to_x):
    total = ready[0]
    for r in (z1, z2, z3):
        total = total + r[1 - info[XHI]].astype(F32)
    to_x[...] = total.astype(BF)


def keep_kernel(info, *refs):
    gated, (weights, z1, z2, z3, x, out_ref) = refs[0:4], refs[4:10]
    acc = product(gated, weights, 4, 2)
    total = acc[:, 0:CB]
    for r in (z1, z2, z3):
        total = total + r[info[XHI]].astype(F32)
    out_ref[:, 0:CB] = total
    out_ref[:, CB : 2 * CB] = acc[:, CB : 2 * CB] + x[0].astype(F32)


def finish_kernel(info, kept, x, z1, z2, z3, out_ref):
    out_ref[:, 0:CB] = (kept[:, 0:CB] + x[...].astype(F32)).astype(BF)
    total = kept[:, CB : 2 * CB]
    for r in (z1, z2, z3):
        total = total + r[0:TOK, :].astype(F32)
    out_ref[:, CB : 2 * CB] = total.astype(BF)


def head_perm(move):
    pairs = []
    for z in range(4):
        for x in range(2):
            for c in range(2):
                z2, x2, c2 = move(z, x, c)
                pairs.append((z * 4 + x * 2 + c, (z2 % 4) * 4 + (x2 % 2) * 2 + c2 % 2))
    return pairs


CORE_SWAP = head_perm(lambda z, x, c: (z, x, c + 1))
X_SWAP = head_perm(lambda z, x, c: (z, x + 1, c))
Z_MOVE = {d: head_perm(lambda z, x, c, d=d: (z + d, x, c)) for d in (1, 2, 3)}
LO_SWAP = [(i, (i + 4) % 8) for i in range(8)]
Y_MOVE = {d: [(x * 4 + y, x * 4 + (y + d) % 4) for x in range(2) for y in range(4)] for d in (1, 2, 3)}


def body(
    queries,
    keys,
    values,
    length,
    mixer_values,
    mixer_keys,
    mixer_queries,
    gate_values,
    step_size,
    decay_rate,
    skip_gain,
    out_weight,
):
    seq = lax.axis_index("seq")
    head = lax.axis_index("head")
    z, x, c = head // 4, (head // 2) % 2, head % 2
    block = lambda zz, xx, half: ((zz % 4) * 4 + (xx % 2) * 2 + c) * 2 + half
    columns = (
        [block(z + d, x + 1, 1) for d in (0, 2, 1, 3)]
        + [block(z + d, i, 0) for d in (1, 2, 3) for i in range(2)]
        + [block(z, x + 1, 0)]
        + [block(z + d, x, 1) for d in (1, 2, 3)]
        + [block(z, x, 0), block(z, x, 1)]
    )
    info = jnp.stack([seq, c, head // 2, length[0], seq % 4, seq // 4, z, x, *columns]).astype(jnp.int32)
    core = lambda a: lax.ppermute(a, "head", CORE_SWAP)
    lo = lambda a: lax.ppermute(a, "seq", LO_SWAP)
    along_y = lambda a, d: lax.ppermute(a, "seq", Y_MOVE[d])
    along_z = lambda a, d: lax.ppermute(a, "head", Z_MOVE[d])

    far_weight = core(out_weight)
    keys, values, mixer_values, mixer_keys = hbm(keys), hbm(values), hbm(mixer_values), hbm(mixer_keys)
    step_size, decay_rate, skip_gain = hbm(step_size), hbm(decay_rate), hbm(skip_gain)

    k_own, vt_own, kv, msg, cum, mv, mk = call(
        prep_kernel,
        info,
        (keys, values, mixer_values, mixer_keys, step_size, decay_rate),
        [HBM, HBM, HBM, HBM, full((HEADS, TOK)), SMEM],
        [VMEM] * 7,
        [kept_shape((TOK, HD), BF)] * 3 + [kept_shape((MSG, HD), BF), kept_shape((16, TOK), F32)] + [kept_shape((TOK, HD), BF)] * 2,
        scratch=[pltpu.VMEM((TOK, HD), BF), pltpu.SemaphoreType.DMA((4,))],
        flops=US,
    )
    from_1, from_3, from_2 = [along_y(msg, d) for d in (1, 3, 2)]
    msgs = [msg, from_1, from_2, from_3]
    kv_far = lo(kv)
    kv_far_other = core(kv_far)

    y_in = call(
        intra_kernel,
        info,
        (cum, hbm(mixer_queries), mk, mv, skip_gain),
        [VMEM, full((TOK, ROWS)), VMEM, VMEM, SMEM],
        VMEM,
        kept_shape((TOK, ROWS), F32),
        flops=US,
    )
    prefix, pdec, total, kv_pair = call(
        combine_kernel,
        info,
        (*msgs, kv, kv_far),
        [VMEM] * 6,
        [VMEM] * 4,
        [kept_shape((ROWS, HD), F32), kept_shape((8, HD), F32), kept_shape((MSG, HD), BF), kept_shape((2 * TOK, HD), BF)],
        flops=US,
        after=(y_in,),
    )
    total_far = lo(total)
    from_1, from_3, from_2 = [along_y(kv_pair, d) for d in (1, 3, 2)]
    from_y = [from_1, from_2, from_3]
    *gated, final_states = call(
        gate_kernel,
        info,
        (cum, mixer_queries, y_in, gate_values, prefix, pdec, total, total_far),
        [VMEM] * 8,
        [VMEM] * 2 + [full((HEADS, HD // 8, NST))],
        [shape((TOK, 2 * HD), BF)] * 2 + [shape((HEADS, HD // 8, NST), F32)],
        flops=US,
    )
    weights = call(
        weights_kernel,
        info,
        (hbm(out_weight), hbm(far_weight)),
        [HBM, HBM],
        VMEM,
        kept_shape((FIRST_BLOCKS, 2 * TOK, CB), BF),
        scratch=[pltpu.SemaphoreType.DMA((2, FIRST_BLOCKS))],
        flops=10**10,
        after=(gated[0],),
    )
    gated += [core(a) for a in gated]

    even_x, odd_x, *to_z = call(
        first_kernel,
        info,
        (*gated, weights),
        [VMEM] * 5,
        [VMEM] * 5,
        [kept_shape((2, TOK, CB), BF)] * 5,
        flops=US,
    )
    even_x, bundle = call(
        bundle_kernel,
        info,
        from_y,
        [VMEM] * 3,
        [ANY, VMEM],
        [kept_shape((2, TOK, CB), BF), kept_shape((3, 2 * TOK, HD), BF)],
        flops=US,
        after=(even_x,),
        alias=0,
    )
    from_even, from_odd = [lax.ppermute(a, "head", X_SWAP) for a in (even_x, odd_x)]
    from_z = [along_z(a, d) for a, d in zip(to_z, Z_FIRST)]

    attended, late, ready = call(
        attend_kernel,
        info,
        (queries, k_own, vt_own, kv_far, kv_far_other, bundle, core(bundle), *gated, hbm(out_weight), hbm(far_weight)),
        [VMEM] * 11 + [HBM] * 2,
        [full((TOK, ROWS)), VMEM, VMEM],
        [shape((TOK, ROWS), BF), kept_shape((LATE_BLOCKS, 2 * TOK, CB), BF), kept_shape((4, TOK, CB), F32)],
        scratch=[pltpu.VMEM((8, TOK, HD), BF)] * 2 + [pltpu.SemaphoreType.DMA((2, LATE_BLOCKS))],
        flops=US,
        limit=28 * 1024 * 1024,
        after=(to_z[0],),
    )
    even_z = call(
        second_even_kernel,
        info,
        (ready, from_even),
        [VMEM] * 2,
        VMEM,
        shape((TOK + 32, CB), BF),
        flops=US,
    )
    from_2 = along_z(even_z, 2)
    odd_z = call(
        second_odd_kernel,
        info,
        (ready, from_odd),
        [VMEM] * 2,
        [VMEM] * 2,
        [shape((TOK, CB), BF)] * 2,
        flops=US,
        after=(even_z,),
    )
    from_z2 = [from_2, *[along_z(a, d) for a, d in zip(odd_z, (1, 3))]]
    to_x2 = call(
        second_x_kernel,
        info,
        (ready, *from_z),
        [VMEM] * 4,
        VMEM,
        shape((TOK, CB), BF),
        flops=US,
        after=(even_z,),
    )
    from_x2 = lax.ppermute(to_x2, "head", X_SWAP)
    kept = call(
        keep_kernel,
        info,
        (*gated, late, *from_z, from_even),
        [VMEM] * 9,
        VMEM,
        shape((TOK, ROWS), F32),
        flops=US,
        after=(to_x2,),
    )
    summed = call(
        finish_kernel,
        info,
        (kept, from_x2, *from_z2),
        [VMEM] * 5,
        full((TOK, ROWS)),
        shape((TOK, ROWS), BF),
        flops=US,
    )
    return (attended, summed, final_states)


def solution(mesh):
    placed = (
        P("seq", "head"),
        P("seq", None),
        P("seq", None),
        P(),
        P("seq", None),
        P("seq", None),
        P("seq", "head"),
        P("seq", "head"),
        P("head", "seq"),
        P("head"),
        P("head"),
        P("head", None),
    )
    return jax.shard_map(
        body,
        mesh=mesh,
        in_specs=placed,
        out_specs=(P("seq", "head"), P("seq", "head"), P("head", "seq", None)),
        check_vma=False,
    )
```

```python
import math

import jax
import jax.numpy as jnp
from jax import lax
from jax.experimental import pallas as pl
from jax.experimental.pallas import tpu as pltpu
from jax.sharding import PartitionSpec as P

H = 64
KVH = 8
HD = 128
NST = 128
TOK = 512
HEADS = 4
ROWS = HEADS * HD
MSG = ROWS + 32
CB = 256
FIRST_BLOCKS = 10
LATE_BLOCKS = 6
Z_FIRST = (2, 1, 3)
Z_SECOND = (2, 1, 3)
BF = jnp.bfloat16
F32 = jnp.float32
US = 10**5
NT = (((1,), (1,)), ((), ()))
VMEM_LIMIT = 16 * 1024 * 1024

SEQ, CORE, GROUP, LENGTH, YPOS, XLO, ZPOS, XHI = range(8)


class Places:
    def __init__(self, ref):
        self.ref = ref

    def __getitem__(self, which):
        if which == LENGTH:
            return self.ref[2]
        if which in (SEQ, YPOS, XLO):
            seq = self.ref[0]
            return {SEQ: seq, YPOS: seq & 3, XLO: seq >> 2}[which]
        head = self.ref[1]
        return {CORE: head & 1, GROUP: head >> 1, ZPOS: head >> 2, XHI: (head >> 1) & 1}[which]


def call(kernel, info, args, in_specs, out_specs, out_shape, grid=(1,), scratch=(), flops=0, nbytes=0, trans=0, extra=(), after=(), limit=VMEM_LIMIT, alias=None):
    scalars = 1 + len(extra)
    first = scalars + len(args)

    def run(*refs):
        kernel(Places(refs[0]), *refs[1:first], *refs[first + len(after) :])

    aliases = {} if alias is None else {first + alias: 0}

    spec = pltpu.PrefetchScalarGridSpec(
        num_scalar_prefetch=scalars,
        grid=grid,
        in_specs=[*in_specs, *[ANY] * len(after)],
        out_specs=out_specs,
        scratch_shapes=list(scratch),
    )
    return pl.pallas_call(
        run,
        grid_spec=spec,
        out_shape=out_shape,
        input_output_aliases=aliases,
        compiler_params=pltpu.CompilerParams(vmem_limit_bytes=limit),
        cost_estimate=pl.CostEstimate(flops=flops, bytes_accessed=nbytes, transcendentals=trans),
    )(info, *extra, *args, *after)


def full(shape):
    return pl.BlockSpec(shape, lambda i, *_: (0,) * len(shape))


def hbm(a):
    return pltpu.with_memory_space_constraint(a, pltpu.HBM)


ANY = pl.BlockSpec(memory_space=pl.ANY)
HBM = pl.BlockSpec(memory_space=pltpu.HBM)
VMEM = pl.BlockSpec(memory_space=pltpu.VMEM)
SMEM = pl.BlockSpec(memory_space=pltpu.SMEM)


def shape(dims, kind):
    return jax.ShapeDtypeStruct(dims, kind)


def kept_shape(dims, kind):
    return pltpu.VMEM(dims, kind)


def split2(a):
    high = a.astype(BF)
    return high, (a - high.astype(F32)).astype(BF)


def prep_kernel(
    info, k_hbm, v_hbm, mv_hbm, mk_hbm, step_ref, rate_ref, k_ref, vt_ref, kv_ref, msg_ref, cum_ref, mv_ref, mk_ref, v_ref, sems
):
    columns = pl.ds(pl.multiple_of(info[GROUP] * HD, HD), HD)
    pairs = ((mv_hbm, mv_ref), (mk_hbm, mk_ref), (k_hbm, k_ref), (v_hbm, v_ref))
    copies = [pltpu.make_async_copy(a.at[:, columns], b, sems.at[i]) for i, (a, b) in enumerate(pairs)]
    for copy in copies:
        copy.start()

    row = lax.broadcasted_iota(jnp.int32, (8, TOK), 0)
    lane = lax.broadcasted_iota(jnp.int32, (8, TOK), 1)
    step = jnp.concatenate([step_ref[...], jnp.zeros((8 - HEADS, TOK), F32)], axis=0)
    step = jnp.where(info[SEQ] * TOK + lane < info[LENGTH], step, 0.0)
    rate = jnp.zeros((8, TOK), F32)
    for h in range(HEADS):
        rate = jnp.where(row == h, rate_ref[h], rate)
    cum = -step * rate
    shift = 1
    while shift < TOK:
        cum = cum + jnp.where(lane >= shift, pltpu.roll(cum, shift, 1), 0.0)
        shift *= 2
    cum_ref[0:8, :] = cum
    cum_ref[8:16, :] = step
    last = cum[:, TOK - 1 : TOK]
    tail = jnp.exp(last - cum) * step
    log = jnp.broadcast_to(last, (8, HD))
    high = log.astype(BF).astype(F32)
    mid = (log - high).astype(BF).astype(F32)
    low = log - high - mid
    msg_ref[ROWS:MSG, :] = jnp.concatenate([high, mid, low, jnp.zeros_like(low)], axis=0).astype(BF)
    copies[0].wait()
    copies[1].wait()
    vt = mv_ref[...].astype(F32).T
    mk = mk_ref[...]
    for h in range(HEADS):
        high, low = split2(vt * tail[h : h + 1, :])
        state = jnp.dot(high, mk, preferred_element_type=F32) + jnp.dot(low, mk, preferred_element_type=F32)
        msg_ref[h * HD : (h + 1) * HD, :] = state.astype(BF)
    copies[2].wait()
    copies[3].wait()
    zero = info[CORE] == 0
    for i in range(TOK // HD):
        part = pl.ds(i * HD, HD)
        turned = v_ref[part, :].astype(F32).T
        vt_ref[part, :] = turned.astype(BF)
        kv_ref[part, :] = jnp.where(zero, k_ref[part, :].astype(F32), turned).astype(BF)


def log_of(msg):
    tail = msg[ROWS:MSG, :].astype(F32)
    return tail[0:8] + tail[8:16] + tail[16:24]


def combine_kernel(info, m0, m1, m2, m3, kv, kv_far, prefix_ref, pdec_ref, total_ref, pair_ref):
    pair_ref[0:TOK, :] = kv[...]
    pair_ref[TOK : 2 * TOK, :] = kv_far[...]
    y = info[YPOS]
    msgs = (m0, m1, m2, m3)
    place = [lax.rem(y - d + 4, 4) for d in range(4)]
    logs = [log_of(m) for m in msgs]
    pre, tot = [], []
    for d in range(4):
        in_pre = jnp.zeros_like(logs[0])
        in_tot = jnp.zeros_like(logs[0])
        for e in range(4):
            if e == d:
                continue
            after = place[e] > place[d]
            in_tot = in_tot + jnp.where(after, logs[e], 0.0)
            in_pre = in_pre + jnp.where(jnp.logical_and(after, place[e] < y), logs[e], 0.0)
        tot.append(jnp.exp(in_tot))
        pre.append(jnp.where(place[d] < y, jnp.exp(in_pre), 0.0))
    whole = logs[0] + logs[1] + logs[2] + logs[3]
    before = jnp.zeros_like(whole)
    for e in range(4):
        before = before + jnp.where(place[e] < y, logs[e], 0.0)
    pdec_ref[...] = jnp.exp(before)
    for h in range(HEADS):
        part = slice(h * HD, (h + 1) * HD)
        own = [m[part, :].astype(F32) for m in msgs]
        total = own[0] * tot[0][h : h + 1]
        prefix = own[1] * pre[1][h : h + 1]
        for d in range(1, 4):
            total = total + own[d] * tot[d][h : h + 1]
        for d in range(2, 4):
            prefix = prefix + own[d] * pre[d][h : h + 1]
        prefix_ref[part, :] = prefix
        total_ref[part, :] = total.astype(BF)
    high = whole.astype(BF).astype(F32)
    mid = (whole - high).astype(BF).astype(F32)
    low = whole - high - mid
    total_ref[ROWS:MSG, :] = jnp.concatenate([high, mid, low, jnp.zeros_like(low)], axis=0).astype(BF)


def intra_kernel(info, cum_ref, c_ref, mk_ref, mv_ref, skip_ref, y_ref):
    cum = cum_ref[0:8, :]
    step = cum_ref[8:16, :]
    cols = cum.T
    half = TOK // 2
    for h in range(HEADS):
        part = slice(h * HD, (h + 1) * HD)
        for i in range(2):
            here = slice(i * half, (i + 1) * half)
            wide = (i + 1) * half
            inner = lax.dot_general(c_ref[here, part], mk_ref[0:wide, :], NT, preferred_element_type=F32)
            t = i * half + lax.broadcasted_iota(jnp.int32, (half, wide), 0)
            s = lax.broadcasted_iota(jnp.int32, (half, wide), 1)
            diff = jnp.where(s <= t, cols[here, h : h + 1] - cum[h : h + 1, 0:wide], -jnp.inf)
            mix = (jnp.exp(diff) * inner * step[h : h + 1, 0:wide]).astype(BF)
            y = jnp.dot(mix, mv_ref[0:wide, :], preferred_element_type=F32)
            y_ref[here, part] = y + skip_ref[h] * mv_ref[here, :].astype(F32)


def gate_kernel(info, cum_ref, c_ref, y_ref, g_ref, prefix_ref, pdec_ref, own_ref, got_ref, out0, out1, fin_ref):
    second = info[XLO] == 1
    ecols = jnp.exp(cum_ref[0:8, :]).T
    for h in range(HEADS):
        part = slice(h * HD, (h + 1) * HD)
        far = pdec_ref[h : h + 1, :] * got_ref[part, :].astype(F32)
        state = prefix_ref[part, :] + jnp.where(second, far, 0.0)
        high, low = split2(state)
        c = c_ref[:, part]
        carried = lax.dot_general(
            jnp.concatenate([c, c], axis=1), jnp.concatenate([high, low], axis=1), NT, preferred_element_type=F32
        )
        y = y_ref[:, part] + ecols[:, h : h + 1] * carried
        g = g_ref[:, part].astype(F32)
        (out0, out1)[h // 2][:, (h % 2) * HD : (h % 2 + 1) * HD] = (y * (g / (1.0 + jnp.exp(-g)))).astype(BF)
    own_log = log_of(own_ref)
    got_log = log_of(got_ref)
    later = jnp.exp(jnp.where(second, own_log, got_log))
    for h in range(HEADS):
        rows = pl.ds(pl.multiple_of(h * HD + info[SEQ] * (HD // 8), HD // 8), HD // 8)
        own = own_ref[rows, :].astype(F32)
        got = got_ref[rows, :].astype(F32)
        first = jnp.where(second, got, own)
        last = jnp.where(second, own, got)
        fin_ref[h] = last + later[h : h + 1, :] * first


SCALE = math.log2(math.e) / math.sqrt(HD)
HALF = TOK // 2
UNITS = [(h, i) for h in range(HEADS) for i in range(2)]
ACC = HD + 16


def with_ones(panels):
    vt = jnp.concatenate(panels, axis=1)
    return jnp.concatenate([vt, jnp.ones((16, vt.shape[1]), BF)], axis=0)


def split_pair(info, mine, other):
    zero = jnp.broadcast_to(info[CORE], mine.shape) == 0
    a, b = mine.astype(F32), other.astype(F32)
    return jnp.where(zero, a, b).astype(BF), jnp.where(zero, b, a).astype(BF)


def pieces(q_ref):
    return [q_ref[i * HALF : (i + 1) * HALF, h * HD : (h + 1) * HD] for h, i in UNITS]


def add_block(queries, k, v, state):
    vt = with_ones([v[i * HD : (i + 1) * HD] for i in range(TOK // HD)])
    scores = [lax.dot_general(k, q, NT, preferred_element_type=F32) for q in queries]
    new = []
    for u in range(len(UNITS)):
        best, summed = state[2 * u], state[2 * u + 1]
        top = jnp.maximum(best, jnp.max(scores[u], axis=0, keepdims=True))
        weights = jnp.exp2((scores[u] - top) * SCALE).astype(BF)
        shrink = jnp.exp2((best - top) * SCALE)
        new += [top, summed * shrink + jnp.dot(vt, weights, preferred_element_type=F32)]
    return tuple(new)


def attend_kernel(
    info, q_ref, k_ref, v_ref, far, far_other, mine, other, g0, g1, g2, g3, near_w, far_w,
    out_ref, late_ref, ready_ref, k_all, v_all, sems,
):
    copies = weight_copies(info, near_w, far_w, late_ref, sems, FIRST_BLOCKS, LATE_BLOCKS)
    for copy in copies:
        copy.start()
    y, x = info[YPOS], info[XLO]
    place = (1 - x) * 4 + y
    k_all[place], v_all[place] = split_pair(info, far[...], far_other[...])
    for d in (1, 2, 3):
        for plane, rows in ((x, slice(0, TOK)), (1 - x, slice(TOK, 2 * TOK))):
            place = plane * 4 + lax.rem(y - d + 4, 4)
            k_all[place], v_all[place] = split_pair(info, mine[d - 1, rows, :], other[d - 1, rows, :])
    limit = info[LENGTH] - info[SEQ] * TOK
    vt = with_ones([v_ref[i * HD : (i + 1) * HD, :] for i in range(TOK // HD)])
    queries = pieces(q_ref)
    state = []
    for u, (h, i) in enumerate(UNITS):
        wide = (i + 1) * HALF
        scores = lax.dot_general(k_ref[0:wide, :], queries[u], NT, preferred_element_type=F32)
        s = lax.broadcasted_iota(jnp.int32, (wide, HALF), 0)
        t = i * HALF + lax.broadcasted_iota(jnp.int32, (wide, HALF), 1)
        keep = jnp.logical_and(s <= t, s < limit)
        scores = jnp.where(keep, scores, -jnp.inf)
        best = jnp.max(scores, axis=0, keepdims=True)
        weights = jnp.exp2((scores - best) * SCALE).astype(BF)
        state += [best, jnp.dot(vt[:, 0:wide], weights, preferred_element_type=F32)]
    state = lax.fori_loop(
        0, info[SEQ], lambda j, state: add_block(queries, k_all[j], v_all[j], state), tuple(state)
    )
    for u, (h, i) in enumerate(UNITS):
        summed = state[2 * u + 1]
        out = summed[0:HD] * (1.0 / summed[HD : HD + 1])
        out_ref[i * HALF : (i + 1) * HALF, h * HD : (h + 1) * HD] = out.T.astype(BF)
    for copy in copies:
        copy.wait()
    for i in range(2):
        acc = product((g0, g1, g2, g3), late_ref, 2 * i, 2)
        ready_ref[2 * i] = acc[:, 0:CB]
        ready_ref[2 * i + 1] = acc[:, CB : 2 * CB]


def column_block(info, k):
    z, x = info[ZPOS], info[XHI]

    def block(zz, xx, half):
        return ((zz & 3) << 3) + ((xx & 1) << 2) + (info[CORE] << 1) + half

    if k < 4:
        return block(k, x + 1, 1)
    if k < 10:
        return block(z + (k - 2) // 2, k % 2, 0)
    if k == 10:
        return block(z, x + 1, 0)
    if k < 14:
        return block(z + k - 10, x, 1)
    return block(z, x, k - 14)


def weight_copies(info, near, far, out_ref, sems, first, n):
    copies = []
    for k in range(n):
        part = pl.ds(pl.multiple_of(column_block(info, first + k) * CB, CB), CB)
        copies += [
            pltpu.make_async_copy(near.at[:, part], out_ref.at[k, 0:TOK, :], sems.at[0, k]),
            pltpu.make_async_copy(far.at[:, part], out_ref.at[k, TOK : 2 * TOK, :], sems.at[1, k]),
        ]
    return copies


def weights_kernel(info, near, far, out_ref, sems):
    copies = weight_copies(info, near, far, out_ref, sems, 0, FIRST_BLOCKS)
    for copy in copies:
        copy.start()
    for copy in copies:
        copy.wait()


def product(gated, weights, first, n):
    g = jnp.concatenate([r[...] for r in gated], axis=1)
    w = jnp.concatenate([weights[first + k] for k in range(n)], axis=1)
    return jnp.dot(g, w, preferred_element_type=F32)


def first_kernel(info, *refs):
    gated, weights, to_x, to_z = refs[0:4], refs[4], refs[5], refs[6:9]
    for i in range(2):
        acc = product(gated, weights, 2 * i, 2).astype(BF)
        to_x[2 * i] = acc[:, 0:CB]
        to_x[2 * i + 1] = acc[:, CB : 2 * CB]
    for out, d in zip(to_z, Z_FIRST):
        acc = product(gated, weights, 2 + 2 * d, 2).astype(BF)
        out[0] = acc[:, 0:CB]
        out[1] = acc[:, CB : 2 * CB]


def bundle_kernel(info, y1, y2, y3, same_ref, bundle_ref):
    for d, r in enumerate((y1, y2, y3)):
        bundle_ref[d] = r[...]


def second_z_kernel(info, ready, x, *to_z):
    for out, d in zip(to_z, Z_SECOND):
        out[...] = (ready[d] + x[lax.rem(info[ZPOS] + d, 4)].astype(F32)).astype(BF)


def second_x_kernel(info, ready, z1, z2, z3, to_x):
    total = ready[0]
    for r in (z1, z2, z3):
        total = total + r[1 - info[XHI]].astype(F32)
    to_x[...] = total.astype(BF)


def keep_kernel(info, *refs):
    gated, (weights, z1, z2, z3, x, out_ref) = refs[0:4], refs[4:10]
    acc = product(gated, weights, 4, 2)
    total = acc[:, 0:CB]
    for r in (z1, z2, z3):
        total = total + r[info[XHI]].astype(F32)
    out_ref[:, 0:CB] = total
    out_ref[:, CB : 2 * CB] = acc[:, CB : 2 * CB] + x[info[ZPOS]].astype(F32)


def finish_kernel(info, kept, x, z1, z2, z3, out_ref):
    out_ref[:, 0:CB] = (kept[:, 0:CB] + x[...].astype(F32)).astype(BF)
    total = kept[:, CB : 2 * CB]
    for r in (z1, z2, z3):
        total = total + r[...].astype(F32)
    out_ref[:, CB : 2 * CB] = total.astype(BF)


def head_perm(move):
    pairs = []
    for z in range(4):
        for x in range(2):
            for c in range(2):
                z2, x2, c2 = move(z, x, c)
                pairs.append((z * 4 + x * 2 + c, (z2 % 4) * 4 + (x2 % 2) * 2 + c2 % 2))
    return pairs


CORE_SWAP = head_perm(lambda z, x, c: (z, x, c + 1))
X_SWAP = head_perm(lambda z, x, c: (z, x + 1, c))
Z_MOVE = {d: head_perm(lambda z, x, c, d=d: (z + d, x, c)) for d in (1, 2, 3)}
LO_SWAP = [(i, (i + 4) % 8) for i in range(8)]
Y_MOVE = {d: [(x * 4 + y, x * 4 + (y + d) % 4) for x in range(2) for y in range(4)] for d in (1, 2, 3)}


def body(
    queries,
    keys,
    values,
    length,
    mixer_values,
    mixer_keys,
    mixer_queries,
    gate_values,
    step_size,
    decay_rate,
    skip_gain,
    out_weight,
):
    seq = lax.axis_index("seq")
    head = lax.axis_index("head")
    info = jnp.stack([seq, head, length[0]]).astype(jnp.int32)
    core = lambda a: lax.ppermute(a, "head", CORE_SWAP)
    lo = lambda a: lax.ppermute(a, "seq", LO_SWAP)
    along_y = lambda a, d: lax.ppermute(a, "seq", Y_MOVE[d])
    along_z = lambda a, d: lax.ppermute(a, "head", Z_MOVE[d])

    far_weight = core(out_weight)
    keys, values, mixer_values, mixer_keys = hbm(keys), hbm(values), hbm(mixer_values), hbm(mixer_keys)
    step_size, decay_rate, skip_gain = hbm(step_size), hbm(decay_rate), hbm(skip_gain)

    k_own, vt_own, kv, msg, cum, mv, mk = call(
        prep_kernel,
        info,
        (keys, values, mixer_values, mixer_keys, step_size, decay_rate),
        [HBM, HBM, HBM, HBM, full((HEADS, TOK)), SMEM],
        [VMEM] * 7,
        [kept_shape((TOK, HD), BF)] * 3 + [kept_shape((MSG, HD), BF), kept_shape((16, TOK), F32)] + [kept_shape((TOK, HD), BF)] * 2,
        scratch=[pltpu.VMEM((TOK, HD), BF), pltpu.SemaphoreType.DMA((4,))],
        flops=US,
    )
    from_1, from_3, from_2 = [along_y(msg, d) for d in (1, 3, 2)]
    msgs = [msg, from_1, from_2, from_3]
    kv_far = lo(kv)
    kv_far_other = core(kv_far)

    y_in = call(
        intra_kernel,
        info,
        (cum, hbm(mixer_queries), mk, mv, skip_gain),
        [VMEM, full((TOK, ROWS)), VMEM, VMEM, SMEM],
        VMEM,
        kept_shape((TOK, ROWS), F32),
        flops=US,
    )
    prefix, pdec, total, kv_pair = call(
        combine_kernel,
        info,
        (*msgs, kv, kv_far),
        [VMEM] * 6,
        [VMEM] * 4,
        [kept_shape((ROWS, HD), F32), kept_shape((8, HD), F32), kept_shape((MSG, HD), BF), kept_shape((2 * TOK, HD), BF)],
        flops=US,
        after=(y_in,),
    )
    total_far = lo(total)
    from_1, from_3, from_2 = [along_y(kv_pair, d) for d in (1, 3, 2)]
    from_y = [from_1, from_2, from_3]
    *gated, final_states = call(
        gate_kernel,
        info,
        (cum, mixer_queries, y_in, gate_values, prefix, pdec, total, total_far),
        [VMEM] * 8,
        [VMEM] * 2 + [full((HEADS, HD // 8, NST))],
        [shape((TOK, 2 * HD), BF)] * 2 + [shape((HEADS, HD // 8, NST), F32)],
        flops=US,
    )
    weights = call(
        weights_kernel,
        info,
        (hbm(out_weight), hbm(far_weight)),
        [HBM, HBM],
        VMEM,
        kept_shape((FIRST_BLOCKS, 2 * TOK, CB), BF),
        scratch=[pltpu.SemaphoreType.DMA((2, FIRST_BLOCKS))],
        flops=10**10,
        after=(gated[0],),
    )
    gated += [core(a) for a in gated]

    to_x, *to_z = call(
        first_kernel,
        info,
        (*gated, weights),
        [VMEM] * 5,
        [VMEM] * 4,
        [kept_shape((4, TOK, CB), BF)] + [kept_shape((2, TOK, CB), BF)] * 3,
        flops=US,
    )
    to_x, bundle = call(
        bundle_kernel,
        info,
        from_y,
        [VMEM] * 3,
        [ANY, VMEM],
        [kept_shape((4, TOK, CB), BF), kept_shape((3, 2 * TOK, HD), BF)],
        flops=US,
        after=(to_x,),
        alias=0,
    )
    from_x = lax.ppermute(to_x, "head", X_SWAP)
    from_z = [along_z(a, d) for a, d in zip(to_z, Z_FIRST)]

    attended, late, ready = call(
        attend_kernel,
        info,
        (queries, k_own, vt_own, kv_far, kv_far_other, bundle, core(bundle), *gated, hbm(out_weight), hbm(far_weight)),
        [VMEM] * 11 + [HBM] * 2,
        [full((TOK, ROWS)), VMEM, VMEM],
        [shape((TOK, ROWS), BF), kept_shape((LATE_BLOCKS, 2 * TOK, CB), BF), kept_shape((4, TOK, CB), F32)],
        scratch=[pltpu.VMEM((8, TOK, HD), BF)] * 2 + [pltpu.SemaphoreType.DMA((2, LATE_BLOCKS))],
        flops=US,
        limit=28 * 1024 * 1024,
        after=(to_z[0],),
    )
    to_z2 = call(
        second_z_kernel,
        info,
        (ready, from_x),
        [VMEM] * 2,
        [VMEM] * 3,
        [shape((TOK, CB), BF)] * 3,
        flops=US,
    )
    from_z2 = [along_z(a, d) for a, d in zip(to_z2, Z_SECOND)]
    to_x2 = call(
        second_x_kernel,
        info,
        (ready, *from_z),
        [VMEM] * 4,
        VMEM,
        shape((TOK, CB), BF),
        flops=US,
        after=(to_z2[0],),
    )
    from_x2 = lax.ppermute(to_x2, "head", X_SWAP)
    kept = call(
        keep_kernel,
        info,
        (*gated, late, *from_z, from_x),
        [VMEM] * 9,
        VMEM,
        shape((TOK, ROWS), F32),
        flops=US,
        after=(to_x2,),
    )
    summed = call(
        finish_kernel,
        info,
        (kept, from_x2, *from_z2),
        [VMEM] * 5,
        full((TOK, ROWS)),
        shape((TOK, ROWS), BF),
        flops=US,
    )
    return (attended, summed, final_states)


def solution(mesh):
    placed = (
        P("seq", "head"),
        P("seq", None),
        P("seq", None),
        P(),
        P("seq", None),
        P("seq", None),
        P("seq", "head"),
        P("seq", "head"),
        P("head", "seq"),
        P("head"),
        P("head"),
        P("head", None),
    )
    return jax.shard_map(
        body,
        mesh=mesh,
        in_specs=placed,
        out_specs=(P("seq", "head"), P("seq", "head"), P("head", "seq", None)),
        check_vma=False,
    )
```
